1024 devices in a mesh: sec: 4 (over z_hi), patch: 32 (over y, x), lev: 8 (over z_lo, core).
Axes of the slice: x: 4, y: 8, z: 16 (z_hi: 4, z_lo: 4; z = z_hi * 4 + z_lo), core: 2. Of those that a mesh axis runs over, the one named last changes fastest.
Arguments:
- atm_tracers: float32 [10, 128, 262144], P(None, 'lev', ('sec', 'patch')), may hold values from -6 to 6
- neighbor_offsets: int32 [3, 262144], P(None, ('sec', 'patch')), may hold values from -2 to 2
- edge_weights: float32 [3, 262144], P(None, ('sec', 'patch')), may hold values from 0.03 to 0.15
- vertical_rates: float32 [10], replicated, may hold values from 0.03 to 0.15
- flux_mixing: float32 [10, 10], replicated, may hold values from -16 to 16
- owners: int32 [262144, 1], P(('sec', 'patch', 'lev')), may hold values from 0 to 31; in each aligned block of 256 rows (0 to 255, 256 to 511, ...) at most 16 rows name the same one
- remap_weights: bfloat16 [512, 262144], P(None, ('sec', 'patch', 'lev')), may hold values from -0.375 to 0.375
- ocean_mask: int32 [262144], P(('sec', 'patch', 'lev')), may hold values 0 or 1
- ocean_state: float32 [2, 80, 262144], P(None, None, ('sec', 'patch', 'lev')), may hold values from -6 to 6
- forcing_mixing: float32 [2, 10], replicated, may hold values from -4 to 4
Outputs:
- atm_out: float32 [10, 128, 262144], P(None, 'lev', ('sec', 'patch'))
- marine_successor_fields: float32 [2, 80, 262144], P(None, None, ('sec', 'patch', 'lev'))
- atm_surface: float32 [262144], P(('sec', 'patch', 'lev'))
The draws below stay inside these ranges and needn't reach their ends.
Inputs may be any that keep to these rules, and one draw needn't show every extreme that they name: `owners`: within the columns of one device, no owner is named by more than 16 columns, a bound that some block reaches.
All inputs are finite; a program needn't handle non-finite values. No bound on the sum of `ocean_mask` on one device may be relied on, other than what follows from the above.
Results may differ from the reference program's by a relative error of at most 0.00035.
Values sent between devices are 32-bit elements; how exact they have to be, the bound alone decides.
A program may use at most 32 MiB of HBM per device.

```python
import math
import jax
import jax.numpy as jnp
import numpy as np
from jax import lax

NTR = 10
ALEV = 128
OLEV = 80
NFLUX = 10
ACOL = 2048
MARINE_GRID_SIZE = 256
HOLDER_ENTRY_MAX = 16
NCOLS = 262144
OTOT = 262144
N_SEC = 4
N_PATCH = 32
N_LEV = 8


def with_ends(values, rng, low, largest):
    dims = values.shape
    index_at = [jax.random.randint(jax.random.fold_in(rng, axis), (), 0, dims[axis]) for axis in range(len(dims))]
    values = values.at[tuple(index_at)].set(low)
    longest = dims.index(max(dims))
    index_at[longest] = (index_at[longest] + 1) % dims[longest]
    return values.at[tuple(index_at)].set(largest)


def steps_of(key, extent, split, least, top_value):
    def one(axis_at, parts):
        heights = jax.random.uniform(jax.random.fold_in(jax.random.fold_in(key, 6), axis_at), (parts,), jnp.float32, least / len(split), top_value / len(split))
        return jnp.repeat(jnp.exp(heights), extent[axis_at] // parts).reshape((-1,) + (1,) * (len(extent) - axis_at - 1))

    loudness = one(*split[0])
    for cut in split[1:]:
        loudness = loudness * one(*cut)
    return loudness


def shared_out(stream_key, own, number, rows, number_of, top, reach, skew):
    sequence = jax.random.permutation(stream_key, number_of)
    packed, ordinary = load_shares(number_of, rows * top, reach, skew, True), load_shares(number_of, rows * top, reach, skew, False)
    places = jnp.arange(number_of)

    def named(tallies, turn):
        used = int((tallies > 0).sum())
        fixed = max(1, used // 4)
        passed = fixed + (places - fixed + turn * (used - fixed)) % max(1, number_of - fixed)
        return jnp.zeros((number_of,), jnp.int32).at[sequence[jnp.where(places < fixed, places, passed)]].set(jnp.asarray(tallies, jnp.int32))

    tallies = jnp.where(number % 4 == 0, named(packed, number // 4), named(ordinary, number - number // 4 - 1))
    mixed = jax.random.permutation(jax.random.fold_in(own, 3), number_of)
    donor, sink = mixed[0:number_of // 2 * 2:2], mixed[1:number_of // 2 * 2:2]
    room = jnp.minimum(tallies[donor] - 1, reach - tallies[sink]) // 2
    room = jnp.where((donor == sequence[0]) | (sink == sequence[0]) | (tallies[sink] == 0), 0, jnp.maximum(room, 0))
    passed = jax.random.randint(jax.random.fold_in(own, 4), (number_of // 2,), 0, 1 << 20) % (room + 1)
    tallies = tallies.at[donor].add(-passed).at[sink].add(passed)
    members = jnp.searchsorted(jnp.cumsum(tallies), jnp.arange(rows * top), side="right").astype(jnp.int32)
    table = members.reshape(top, rows).T
    table = table[jax.random.permutation(jax.random.fold_in(own, 1), rows)]
    turn = jax.random.randint(jax.random.fold_in(own, 2), (rows, 1), 0, top)
    return jnp.take_along_axis(table, (jnp.arange(top)[None, :] + turn) % top, axis=1)


def load_shares(count, total, most, skew, full):
    weights = [(1 << 20) // math.isqrt(rank ** skew) + 1 for rank in range(1, count + 1)]
    largest = most if full else min(most, max(-(-total // count), total * weights[0] // sum(weights)))
    least = 1 if total - largest >= count - 1 else 0
    counts, surplus = [largest] + [least] * (count - 1), total - largest - least * (count - 1)
    while surplus > 0:
        candidates = [i for i in range(1, count) if counts[i] < largest] or [i for i in range(1, count) if counts[i] < most]
        mass, remaining = sum([weights[i] for i in candidates]), surplus
        for i in candidates:
            more = min(most - counts[i], max(1, remaining * weights[i] // mass), surplus)
            counts[i] = counts[i] + more
            surplus = surplus - more
    return np.array(counts)


def scatter_about(stream_key, extent, scale, limit, cuts=(), kind=jnp.bfloat16):
    drawn = jax.random.normal(stream_key, extent, jnp.float32) * scale
    if len(cuts) > 0:
        drawn = steps_of(stream_key, extent, cuts, -0.22, 0.18) * drawn
    return jnp.clip(drawn, min=-limit, max=limit).astype(kind)


def setup_inputs(seed: int = 0) -> dict:
    arg_keys = jax.random.split(jax.random.key(seed), 11)
    atm_tracers = scatter_about(arg_keys[0], (NTR, ALEV, NCOLS), 1.0, 6.0, ((1, 8), (2, 128)), jnp.float32)
    neighbor_offsets = with_ends(jax.random.randint(arg_keys[1], (3, NCOLS), -2, 3), jax.random.fold_in(arg_keys[1], 1), -2, 2).astype(jnp.int32)
    edge_weights = jnp.clip(jnp.exp(math.log(0.15) - 1.609438 * jax.random.uniform(arg_keys[2], (3, NCOLS), jnp.float32) ** steps_of(arg_keys[2], (3, NCOLS), ((1, 128),), -0.2, 0.2)), 0.03, 0.15)
    vertical_rates = jnp.clip(jnp.exp(jax.random.uniform(arg_keys[3], (NTR,), jnp.float32, math.log(0.03), math.log(0.15))), 0.03, 0.15)
    flux_mixing = scatter_about(arg_keys[4], (NFLUX, NTR), 4.0, 16.0, (), jnp.float32)
    owners_keys = jax.random.split(jax.random.fold_in(arg_keys[5], 1), NCOLS // (ACOL // N_LEV))
    owners_turns = jax.random.permutation(jax.random.fold_in(arg_keys[5], 3), NCOLS // (ACOL // N_LEV))
    owners = jax.vmap(lambda own, number: shared_out(jax.random.fold_in(arg_keys[5], 2), own, number, ACOL // N_LEV, N_PATCH, 1, HOLDER_ENTRY_MAX, 2))(owners_keys, owners_turns).reshape((NCOLS, 1))
    remap_weights = scatter_about(arg_keys[6], (N_PATCH * HOLDER_ENTRY_MAX, OTOT), (N_PATCH * HOLDER_ENTRY_MAX // 2) ** -0.5, 0.375, ((1, 1024),))
    ocean_mask = with_ends((jax.random.randint(arg_keys[7], (OTOT,), 0, 4) < 3).astype(jnp.int32), jax.random.fold_in(arg_keys[7], 1), 0, 1)
    ocean_state = scatter_about(arg_keys[8], (2, OLEV, OTOT), 1.0, 6.0, ((2, 1024),), jnp.float32)
    forcing_mixing = scatter_about(arg_keys[9], (2, NFLUX), 0.5, 4.0, (), jnp.float32)
    return {"atm_tracers": atm_tracers, "neighbor_offsets": neighbor_offsets, "edge_weights": edge_weights, "vertical_rates": vertical_rates, "flux_mixing": flux_mixing, "owners": owners, "remap_weights": remap_weights, "ocean_mask": ocean_mask, "ocean_state": ocean_state, "forcing_mixing": forcing_mixing}


def atm_step(q, offsets, edge_weights, vertical_rates):
    ncol = q.shape[2]
    cols = jnp.arange(ncol, dtype=jnp.int32)
    result = q
    for j in range(3):
        index = jnp.mod(cols + offsets[j], ncol).astype(jnp.int32)
        result = result + edge_weights[j][None, None, :] * (jnp.take(q, index, axis=2) - q)
    levels = jnp.arange(ALEV, dtype=jnp.int32)
    for m in (-2, -1, 1, 2):
        beside = jnp.roll(q, -m, axis=1)
        valid = ((levels + m >= 0) & (levels + m < ALEV)).astype(jnp.float32)
        factor = 1.0 if abs(m) == 1 else 0.5
        result = result + (vertical_rates * factor)[:, None, None] * (beside - q) * valid[None, :, None]
    return result


def ocean_step(state, forcing):
    levels = jnp.arange(OLEV, dtype=jnp.int32)
    profile = jnp.exp(-levels.astype(jnp.float32) / 8.0)
    result = state + profile[None, :, None] * forcing[:, None, :]
    for m in (-1, 1):
        beside = jnp.roll(state, -m, axis=1)
        valid = ((levels + m >= 0) & (levels + m < OLEV)).astype(jnp.float32)
        result = result + 0.2 * (beside - state) * valid[None, :, None]
    return result


def reference(atm_tracers, neighbor_offsets, edge_weights, vertical_rates, flux_mixing, owners, remap_weights, ocean_mask, ocean_state, forcing_mixing):
    fine_arithmetic_mode = lax.Precision.HIGHEST
    q = atm_tracers
    for step in range(2):
        q = atm_step(q, neighbor_offsets, edge_weights, vertical_rates)
    colmean = jnp.sum(q, axis=1) / ALEV
    flux = jnp.tanh(jnp.dot(flux_mixing, colmean, precision=fine_arithmetic_mode))
    accelerator_roster = N_SEC * N_PATCH * N_LEV
    block = ACOL // N_LEV
    owned = owners[:, 0].reshape(accelerator_roster, block)
    patch_groups = jnp.arange(N_PATCH, dtype=jnp.int32)
    onehot = (owned[:, :, None] == patch_groups[None, None, :]).astype(jnp.int32)
    rank = jnp.cumsum(onehot, axis=1) - onehot
    slot = jnp.sum(rank * onehot, axis=2).astype(jnp.int32)
    source = jnp.arange(accelerator_roster, dtype=jnp.int32)
    sec_of = source // (N_PATCH * N_LEV)
    patch_of = (source // N_LEV) % N_PATCH
    lev_of = source % N_LEV
    dest = ((sec_of[:, None] * N_PATCH + owned) * N_LEV + lev_of[:, None]).astype(jnp.int32)
    patch_src = jnp.broadcast_to(patch_of[:, None], dest.shape).astype(jnp.int32)
    flux_t = jnp.transpose(flux).reshape(accelerator_roster, block, NFLUX)
    recv = jnp.zeros((accelerator_roster, N_PATCH, HOLDER_ENTRY_MAX, NFLUX), jnp.float32).at[dest, patch_src, slot].set(flux_t)
    recv = recv.reshape(accelerator_roster, N_PATCH * HOLDER_ENTRY_MAX, NFLUX)
    regrid_operator = remap_weights.astype(jnp.float32).reshape(N_PATCH * HOLDER_ENTRY_MAX, accelerator_roster, MARINE_GRID_SIZE)
    real_valued_filter = ocean_mask.astype(jnp.float32).reshape(accelerator_roster, MARINE_GRID_SIZE)
    oflux = jnp.einsum('dsf,sdc->dfc', recv, regrid_operator, precision=fine_arithmetic_mode) * real_valued_filter[:, None, :]
    oflux = jnp.transpose(oflux, (1, 0, 2)).reshape(NFLUX, accelerator_roster * MARINE_GRID_SIZE)
    forcing = jnp.dot(forcing_mixing, oflux, precision=fine_arithmetic_mode)
    marine_successor_fields = ocean_step(ocean_state, forcing)
    marine_skin_warmth = marine_successor_fields[0, 0, :].reshape(accelerator_roster, MARINE_GRID_SIZE) * real_valued_filter
    gathered_exchange_rates = jnp.einsum('cpz,pz->pc', regrid_operator, marine_skin_warmth, precision=fine_arithmetic_mode).reshape(accelerator_roster, N_PATCH, HOLDER_ENTRY_MAX)
    atm_surface = gathered_exchange_rates[dest, patch_src, slot].reshape(accelerator_roster * block)
    return q, marine_successor_fields, atm_surface
```

```python
import functools
import jax
import jax.numpy as jnp
from jax import lax
from jax.experimental import pallas as pl
from jax.experimental.pallas import tpu as pltpu
from jax.sharding import PartitionSpec as P

F32 = jnp.float32
BF16 = jnp.bfloat16
MESH = pl.DeviceIdType.MESH
DELTAS = (-2, -1, 1, 2)
LANES = 128
HALO = 4


def split_2(x):
    high = x.astype(BF16)
    return high, (x - high.astype(F32)).astype(BF16)


def interval(
    dims,
    atm, offs, edge, rates, mixing, owners, weights, mask, ocean, forcing_mix,
    atm_out, ocean_out, surface_out,
    ring, step1, result, coef, offs_v, edge_v, rates_s, mix_v, owners_v, weights_v, mask_v, ocean_v, base_v, fmix_v,
    edge_send, edge_recv, sums_a, sums_b, got_a, got_b, flux_send, flux_recv, back_send, back_recv, surface_v,
    cols_hot, slot_hot, mix_cols,
    atm_sem, in_sem, edge_sem, lev_send_sem, lev_up_sem, lev_down_sem, sum_sem, flux_sem, back_sem, out_sem,
):
    n_sec, n_patch, n_lev = dims
    ntr, klev, ncol = atm.shape
    alev = klev * n_lev
    block = ncol // n_lev
    slots = weights.shape[0] // n_patch
    copies = LANES // slots
    wide = ncol + 2 * LANES
    rows = klev + 2 * HALO

    sec, patch, lev = lax.axis_index("sec"), lax.axis_index("patch"), lax.axis_index("lev")
    place = sec * n_patch + patch
    n_place = n_sec * n_patch

    def column_neighbour(step):
        other = lax.rem(place + step + n_place, n_place)
        return lax.div(other, n_patch), lax.rem(other, n_patch)

    left, right = column_neighbour(-1), column_neighbour(1)

    def level_of(step):
        return lax.rem(lev + step + n_lev, n_lev)

    small = [
        (offs, offs_v), (edge, edge_v), (rates, rates_s), (owners, owners_v),
        (mixing, mix_v), (forcing_mix, fmix_v), (mask, mask_v), (ocean, ocean_v), (weights, weights_v),
    ]
    loads = [pltpu.make_async_copy(a, b, in_sem.at[i]) for i, (a, b) in enumerate(small)]
    for i in (0, 1):
        loads[i].start()
    atm_loads = [
        pltpu.make_async_copy(atm.at[t], ring.at[t, 0:klev, LANES : LANES + ncol], atm_sem.at[t])
        for t in range(ntr)
    ]
    for load in atm_loads:
        load.start()
    for load in loads[2:]:
        load.start()

    barrier = pltpu.get_barrier_semaphore()

    def greet(where):
        pl.semaphore_signal(barrier, inc=1, device_id=where, device_id_type=MESH)

    for step in (-1, 0, 1):
        for s, p in (left, right):
            greet((s, p, level_of(step)))
    for i in range(1, n_lev):
        greet((sec, patch, level_of(i)))

    def greet_patch(i, carry):
        greet((sec, lax.rem(patch + i, n_patch), lev))
        return carry

    lax.fori_loop(1, n_patch, greet_patch, 0)

    loads[0].wait()
    loads[1].wait()
    offsets, exchange = offs_v[...], edge_v[...]
    total = jnp.zeros((1, ncol), F32)
    for i, delta in enumerate(DELTAS):
        part = jnp.sum(jnp.where(offsets == delta, exchange, 0.0), axis=0, keepdims=True)
        total = total + part
        coef[i, :, LANES : LANES + ncol] = jnp.broadcast_to(part, (8, ncol))
    coef[4, :, LANES : LANES + ncol] = jnp.broadcast_to(1.0 - total, (8, ncol))

    lane = lax.broadcasted_iota(jnp.int32, (8, LANES), 1)
    row = lax.broadcasted_iota(jnp.int32, (8, LANES), 0)
    coef_lane = 2 * ntr * HALO
    for load in atm_loads:
        load.wait()
    first = jnp.zeros((8, LANES), F32)
    last = jnp.zeros((8, LANES), F32)
    for t in range(ntr):
        for k in range(2):
            at = (2 * t + k) * HALO
            here = (lane >= at) & (lane < at + HALO)
            a = ring[t, 8 * k : 8 * k + 8, LANES : 2 * LANES]
            b = ring[t, 8 * k : 8 * k + 8, ncol : ncol + LANES]
            first = jnp.where(here, pltpu.roll(a, at, 1) if at else a, first)
            last = jnp.where(here, pltpu.roll(b, at + HALO, 1), last)
    here = (lane >= coef_lane) & (lane < coef_lane + HALO)
    for i in range(4):
        a = coef[i, :, LANES : 2 * LANES]
        b = coef[i, :, ncol : ncol + LANES]
        first = jnp.where(here & (row == i), pltpu.roll(a, coef_lane, 1), first)
        last = jnp.where(here & (row == i), pltpu.roll(b, coef_lane + HALO, 1), last)
    edge_send[0] = first
    edge_send[1] = last

    pl.semaphore_wait(barrier, 6 + (n_lev - 1) + (n_patch - 1))

    for side, (s, p) in ((0, right), (1, left)):
        for step in (0, -1, 1):
            pltpu.make_async_remote_copy(
                src_ref=edge_send.at[1 - side],
                dst_ref=edge_recv.at[side, 1 - step],
                send_sem=edge_sem.at[0],
                recv_sem=edge_sem.at[1],
                device_id=(s, p, level_of(step)),
                device_id_type=MESH,
            ).start()

    def to_lower(t):
        return pltpu.make_async_remote_copy(
            src_ref=atm.at[t, 0:HALO, :],
            dst_ref=ring.at[t, klev : klev + HALO, LANES : LANES + ncol],
            send_sem=lev_send_sem.at[0, t],
            recv_sem=lev_up_sem.at[t],
            device_id=(sec, patch, level_of(-1)),
            device_id_type=MESH,
        )

    def to_upper(t):
        return pltpu.make_async_remote_copy(
            src_ref=atm.at[t, klev - HALO : klev, :],
            dst_ref=ring.at[t, klev + HALO : rows, LANES : LANES + ncol],
            send_sem=lev_send_sem.at[1, t],
            recv_sem=lev_down_sem.at[t],
            device_id=(sec, patch, level_of(1)),
            device_id_type=MESH,
        )

    @pl.when(lev > 0)
    def _():
        for t in range(ntr):
            to_lower(t).start()

    @pl.when(lev < n_lev - 1)
    def _():
        for t in range(ntr):
            to_upper(t).start()

    @pl.when(lev == 0)
    def _():
        ring[:, klev + HALO : rows, LANES : LANES + ncol] = jnp.zeros((ntr, HALO, ncol), F32)

    @pl.when(lev == n_lev - 1)
    def _():
        ring[:, klev : klev + HALO, LANES : LANES + ncol] = jnp.zeros((ntr, HALO, ncol), F32)

    for load in loads[2:]:
        load.wait()
    owned = owners_v[...]
    hot = (lax.broadcasted_iota(jnp.int32, (n_patch, block), 0) == owned).astype(F32)
    cols_hot[...] = hot
    earlier = (
        lax.broadcasted_iota(jnp.int32, (block, block), 0) < lax.broadcasted_iota(jnp.int32, (block, block), 1)
    ).astype(F32).astype(BF16)
    rank = jnp.dot(hot.astype(BF16), earlier, preferred_element_type=F32)
    slot = jnp.sum(rank * hot, axis=0, keepdims=True).astype(jnp.int32)
    lane_slot = lax.rem(lax.broadcasted_iota(jnp.int32, (LANES, block), 0), slots)
    slot_hot[...] = (lane_slot == slot).astype(F32).astype(BF16)
    for t in range(ntr):
        mix_cols[t] = jnp.broadcast_to(mix_v[:, t : t + 1], (mixing.shape[0], block))

    state = ocean_v[...]
    nol = state.shape[1]
    level = lax.broadcasted_iota(jnp.int32, state.shape, 1)
    above = jnp.where(level < nol - 1, pltpu.roll(state, nol - 1, 1) - state, 0.0)
    below = jnp.where(level > 0, pltpu.roll(state, 1, 1) - state, 0.0)
    base_v[...] = state + 0.2 * above + 0.2 * below

    pltpu.make_async_copy(edge_recv, edge_recv, edge_sem.at[1]).wait()
    beside = jnp.where(
        lane < LANES // 2,
        pltpu.roll(edge_recv[1, 1], LANES - coef_lane, 1),
        pltpu.roll(edge_recv[0, 1], LANES - HALO - coef_lane, 1),
    )
    total = jnp.zeros((1, LANES), F32)
    for i in range(4):
        part = beside[i : i + 1, :]
        total = total + part
        for at in (0, LANES + ncol):
            coef[i, :, at : at + LANES] = jnp.broadcast_to(part, (8, LANES))
    for at in (0, LANES + ncol):
        coef[4, :, at : at + LANES] = jnp.broadcast_to(1.0 - total, (8, LANES))

    ring_row = lax.broadcasted_iota(jnp.int32, (rows, LANES), 0)
    k = lev * klev + jnp.where(ring_row < klev + HALO, ring_row, ring_row - rows)
    inside = (k >= 0) & (k < alev)
    vertical = (
        3.0
        - (k < 1).astype(F32) - 0.5 * (k < 2).astype(F32)
        - (k > alev - 2).astype(F32) - 0.5 * (k > alev - 3).astype(F32)
    )
    inside_halo = inside[klev:, :]

    def across(x, times):
        return jnp.concatenate([x] * times, axis=1) if times > 1 else x

    def down(x):
        return jnp.concatenate([x] * (rows // 8), axis=0)

    def stencil(x, at, tiles, rate, rate_vertical):
        width = tiles * LANES
        middle = x[:, LANES : LANES + width]
        out = middle * (down(coef[4, :, at : at + width]) - across(rate_vertical, tiles))
        for i, delta in enumerate(DELTAS):
            moved = pltpu.roll(x, (-delta) % x.shape[1], 1)[:, LANES : LANES + width]
            out = out + down(coef[i, :, at : at + width]) * moved
        one = pltpu.roll(middle, 1, 0) + pltpu.roll(middle, rows - 1, 0)
        two = pltpu.roll(middle, 2, 0) + pltpu.roll(middle, rows - 2, 0)
        return out + rate * (one + 0.5 * two)

    def masked(x, tiles):
        return jnp.concatenate(
            [x[:klev], jnp.where(across(inside_halo, tiles), x[klev:], 0.0)], axis=0
        )

    tiles = 4
    chunk = tiles * LANES

    def tracer(t, sums, at_row):
        @pl.when(lev < n_lev - 1)
        def _():
            to_lower(t).wait_recv()

        @pl.when(lev > 0)
        def _():
            to_upper(t).wait_recv()

        rate = rates_s[t]
        rate_vertical = rate * vertical
        low, high = 2 * HALO * t, 2 * HALO * t + HALO

        def sides(from_left, from_right, lanes_at):
            return jnp.where(
                lane < LANES // 2,
                pltpu.roll(from_right, lax.rem(LANES - lanes_at, LANES), 1),
                pltpu.roll(from_left, LANES - HALO - lanes_at, 1),
            )

        corner = jnp.where(
            row < HALO,
            sides(edge_recv[0, 2], edge_recv[1, 2], low),
            sides(edge_recv[0, 0], edge_recv[1, 0], high),
        )
        halo = jnp.concatenate(
            [
                sides(edge_recv[0, 1], edge_recv[1, 1], low),
                sides(edge_recv[0, 1], edge_recv[1, 1], high),
                jnp.where(inside_halo, corner, 0.0),
            ],
            axis=0,
        )
        ring[t, :, 0:LANES] = halo
        ring[t, :, LANES + ncol : wide] = halo

        x = jnp.concatenate([ring[t, :, ncol : ncol + LANES], halo, ring[t, :, LANES : 2 * LANES]], axis=1)
        halo = masked(stencil(x, 0, 1, rate, rate_vertical), 1)
        step1[:, 0:LANES] = halo
        step1[:, LANES + ncol : wide] = halo
        for c in range(ncol // chunk):
            at = LANES + c * chunk
            x = ring[t, :, at - LANES : at + chunk + LANES]
            step1[:, at : at + chunk] = masked(stencil(x, at, tiles, rate, rate_vertical), tiles)
        for c in range(ncol // chunk):
            at = LANES + c * chunk
            x = step1[:, at - LANES : at + chunk + LANES]
            out = stencil(x, at, tiles, rate, rate_vertical)[:klev]
            result[t, :, c * chunk : (c + 1) * chunk] = out
            column_sums = jnp.sum(out, axis=0, keepdims=True)
            for i in range(chunk // block):
                sums[c * (chunk // block) + i, pl.ds(at_row, 1), :] = column_sums[:, i * block : (i + 1) * block]
        pltpu.make_async_copy(result.at[t], atm_out.at[t], out_sem.at[0]).start()

    n_a = sums_a.shape[1]

    def send_sums(sums, got, which):
        for i in range(1, n_lev):
            pltpu.make_async_remote_copy(
                src_ref=sums.at[level_of(i)],
                dst_ref=got.at[n_lev - 1 - i],
                send_sem=sum_sem.at[0, which],
                recv_sem=sum_sem.at[1, which],
                device_id=(sec, patch, level_of(i)),
                device_id_type=MESH,
            ).start()

    def tracer_a(t, carry):
        tracer(t, sums_a, t)
        return carry

    def tracer_b(t, carry):
        tracer(t, sums_b, t - n_a)
        return carry

    lax.fori_loop(0, n_a, tracer_a, 0)
    send_sums(sums_a, got_a, 0)
    lax.fori_loop(n_a, ntr, tracer_b, 0)
    send_sums(sums_b, got_b, 1)

    pick = (
        lax.broadcasted_iota(jnp.int32, (ntr, ntr), 0) == lax.broadcasted_iota(jnp.int32, (ntr, ntr), 1)
    )
    fmix = fmix_v[...]
    fmix_cols = [
        jnp.sum(jnp.where(pick, jnp.broadcast_to(fmix[v : v + 1, :], (ntr, ntr)), 0.0), axis=1, keepdims=True)
        for v in range(2)
    ]

    def level_sums(sums, got, which):
        pltpu.make_async_copy(got, got, sum_sem.at[1, which]).wait()
        out = sums[lev]
        for i in range(n_lev - 1):
            out = out + got[i]
        return out

    mean_a = level_sums(sums_a, got_a, 0) * (1.0 / alev)
    mixed = jnp.zeros((mixing.shape[0], block), F32)
    for t in range(n_a):
        mixed = mixed + mix_cols[t] * mean_a[t : t + 1, :]
    mean_b = level_sums(sums_b, got_b, 1) * (1.0 / alev)
    for t in range(n_a, ntr):
        mixed = mixed + mix_cols[t] * mean_b[t - n_a : t - n_a + 1, :]
    flux = jnp.tanh(mixed)
    hot = cols_hot[...]
    parts = []
    for v in range(2):
        forced = jnp.sum(fmix_cols[v] * flux, axis=0, keepdims=True)
        parts += [(hot * piece.astype(F32)).astype(BF16) for piece in split_2(forced)]
    slot_map = slot_hot[...]
    out = lax.dot_general(
        jnp.concatenate(parts, axis=0), slot_map, (((1,), (1,)), ((), ())), preferred_element_type=F32
    )
    outgoing = [out[2 * v * n_patch : (2 * v + 1) * n_patch] + out[(2 * v + 1) * n_patch : (2 * v + 2) * n_patch] for v in range(2)]
    for v in range(2):
        flux_send[:, v * LANES : (v + 1) * LANES] = outgoing[v]

    def send_flux(i, carry):
        other = lax.rem(patch + i, n_patch)
        pltpu.make_async_remote_copy(
            src_ref=flux_send.at[pl.ds(other, 1), :],
            dst_ref=flux_recv.at[pl.ds(patch, 1), :],
            send_sem=flux_sem.at[0],
            recv_sem=flux_sem.at[1],
            device_id=(sec, other, lev),
            device_id_type=MESH,
        ).start()
        return carry

    lax.fori_loop(1, n_patch, send_flux, 0)
    own_row = pl.ds(patch, 1)
    pltpu.make_async_copy(flux_send.at[own_row, :], flux_recv.at[own_row, :], flux_sem.at[1]).start()
    ocean_cells = mask_v[...].astype(F32)
    pltpu.make_async_copy(flux_recv, flux_recv, flux_sem.at[1]).wait()

    groups = n_patch * slots // LANES
    received = []
    for v in range(2):
        pieces = []
        for g in range(groups):
            tile = flux_recv[g * copies : (g + 1) * copies, v * LANES : (v + 1) * LANES]
            pieces.append(jnp.sum(jnp.where(lax.div(lane, slots) == row, tile, 0.0), axis=0, keepdims=True))
        received.append(jnp.concatenate(pieces, axis=1))
    w = weights_v[...]

    def stacked(values):
        at = lax.broadcasted_iota(jnp.int32, (16, values[0].shape[1]), 0)
        out = jnp.zeros((16, values[0].shape[1]), F32)
        for i, value in enumerate(values):
            out = jnp.where(at == i, value.astype(F32), out)
        return out.astype(BF16)

    sums = jnp.dot(stacked([*split_2(received[0]), *split_2(received[1])]), w, preferred_element_type=F32)
    forcing = [(sums[2 * v : 2 * v + 1] + sums[2 * v + 1 : 2 * v + 2]) * ocean_cells for v in range(2)]
    warmth = (base_v[0, 0:1, :] + forcing[0]) * ocean_cells
    back = lax.dot_general(
        stacked([*split_2(warmth)]), w, (((1,), (1,)), ((), ())), preferred_element_type=F32
    )
    back = back[0:1] + back[1:2]
    for g in range(groups):
        back_send[g : g + 1, :] = back[:, g * LANES : (g + 1) * LANES]

    def send_back(i, carry):
        other = lax.rem(patch + i, n_patch)
        pltpu.make_async_remote_copy(
            src_ref=back_send.at[pl.ds(lax.div(other, copies), 1), :],
            dst_ref=back_recv.at[pl.ds(patch, 1), :],
            send_sem=back_sem.at[0],
            recv_sem=back_sem.at[1],
            device_id=(sec, other, lev),
            device_id_type=MESH,
        ).start()
        return carry

    lax.fori_loop(1, n_patch, send_back, 0)
    pltpu.make_async_copy(
        back_send.at[pl.ds(lax.div(patch, copies), 1), :], back_recv.at[own_row, :], back_sem.at[1]
    ).start()

    depth = lax.broadcasted_iota(jnp.int32, (nol, block), 0).astype(F32)
    profile = jnp.exp(-depth / 8.0)
    for v in range(2):
        ocean_v[v] = base_v[v] + profile * forcing[v]
    pltpu.make_async_copy(ocean_v, ocean_out, out_sem.at[1]).start()

    pltpu.make_async_copy(back_recv, back_recv, back_sem.at[1]).wait()
    at_lane = lax.broadcasted_iota(jnp.int32, (n_patch, LANES), 1)
    own = lax.div(at_lane, slots) == lax.rem(patch, copies)
    returned = jnp.where(own, back_recv[...], 0.0)
    values = jnp.dot(jnp.concatenate(split_2(returned), axis=0), slot_map, preferred_element_type=F32)
    surface_v[...] = jnp.sum((values[:n_patch] + values[n_patch:]) * hot, axis=0, keepdims=True)
    pltpu.make_async_copy(surface_v, surface_out, out_sem.at[2]).start()

    six = edge_recv
    pltpu.make_async_copy(six, six, edge_sem.at[0]).wait()

    @pl.when(lev > 0)
    def _():
        for t in range(ntr):
            to_lower(t).wait_send()

    @pl.when(lev < n_lev - 1)
    def _():
        for t in range(ntr):
            to_upper(t).wait_send()

    pltpu.make_async_copy(got_a, got_a, sum_sem.at[0, 0]).wait()
    pltpu.make_async_copy(got_b, got_b, sum_sem.at[0, 1]).wait()
    count = n_patch // 2
    while count:
        for ref, sem in ((flux_recv, flux_sem), (back_recv, back_sem)):
            some = ref.at[pl.ds(0, count), :]
            pltpu.make_async_copy(some, some, sem.at[0]).wait()
        count //= 2
    pltpu.make_async_copy(result, atm_out, out_sem.at[0]).wait()
    pltpu.make_async_copy(ocean_v, ocean_out, out_sem.at[1]).wait()
    pltpu.make_async_copy(surface_v, surface_out, out_sem.at[2]).wait()


def solution(mesh):
    dims = tuple(mesh.shape[a] for a in ("sec", "patch", "lev"))
    n_sec, n_patch, n_lev = dims

    def per_device(atm, offs, edge, rates, mixing, owners, weights, mask, ocean, forcing_mix):
        ntr, klev, ncol = atm.shape
        rows, wide = klev + 2 * HALO, ncol + 2 * LANES
        block = ncol // n_lev
        nflux = mixing.shape[0]
        owners, mask = owners.reshape(1, -1), mask.reshape(1, -1)
        dma = pltpu.SemaphoreType.DMA
        vmem = pltpu.VMEM
        any_space = pl.BlockSpec(memory_space=pl.ANY)
        out = pl.pallas_call(
            functools.partial(interval, dims),
            out_shape=(
                jax.ShapeDtypeStruct(atm.shape, F32),
                jax.ShapeDtypeStruct(ocean.shape, F32),
                jax.ShapeDtypeStruct((1, block), F32),
            ),
            in_specs=[any_space] * 10,
            out_specs=(any_space,) * 3,
            scratch_shapes=[
                vmem((ntr, rows, wide), F32),
                vmem((rows, wide), F32),
                vmem(atm.shape, F32),
                vmem((5, 8, wide), F32),
                vmem(offs.shape, jnp.int32),
                vmem(edge.shape, F32),
                pltpu.SMEM(rates.shape, F32),
                vmem(mixing.shape, F32),
                vmem(owners.shape, jnp.int32),
                vmem(weights.shape, BF16),
                vmem(mask.shape, jnp.int32),
                vmem(ocean.shape, F32),
                vmem(ocean.shape, F32),
                vmem(forcing_mix.shape, F32),
                vmem((2, 8, LANES), F32),
                vmem((2, 3, 8, LANES), F32),
                vmem((n_lev, 8, block), F32),
                vmem((n_lev, ntr - 8, block), F32),
                vmem((n_lev - 1, 8, block), F32),
                vmem((n_lev - 1, ntr - 8, block), F32),
                vmem((n_patch, 2 * LANES), F32),
                vmem((n_patch, 2 * LANES), F32),
                vmem((weights.shape[0] // LANES, LANES), F32),
                vmem((n_patch, LANES), F32),
                vmem((1, block), F32),
                vmem((n_patch, block), F32),
                vmem((LANES, block), BF16),
                vmem((ntr, nflux, block), F32),
                dma((ntr,)),
                dma((9,)),
                dma((2,)),
                dma((2, ntr)),
                dma((ntr,)),
                dma((ntr,)),
                dma((2, 2)),
                dma((2,)),
                dma((2,)),
                dma((3,)),
            ],
            compiler_params=pltpu.CompilerParams(
                collective_id=0, has_side_effects=True, vmem_limit_bytes=32 * 1024 * 1024
            ),
            name="interval",
        )(atm, offs, edge, rates, mixing, owners, weights, mask, ocean, forcing_mix)
        return out[0], out[1], out[2].reshape(-1)

    in_specs = (
        P(None, "lev", ("sec", "patch")),
        P(None, ("sec", "patch")),
        P(None, ("sec", "patch")),
        P(),
        P(),
        P(("sec", "patch", "lev"), None),
        P(None, ("sec", "patch", "lev")),
        P(("sec", "patch", "lev")),
        P(None, None, ("sec", "patch", "lev")),
        P(),
    )
    out_specs = (
        P(None, "lev", ("sec", "patch")),
        P(None, None, ("sec", "patch", "lev")),
        P(("sec", "patch", "lev")),
    )
    return jax.shard_map(per_device, mesh=mesh, in_specs=in_specs, out_specs=out_specs, check_vma=False)
```

```python
import functools
import jax
import jax.numpy as jnp
from jax import lax
from jax.experimental import pallas as pl
from jax.experimental.pallas import tpu as pltpu
from jax.sharding import PartitionSpec as P

F32 = jnp.float32
BF16 = jnp.bfloat16
MESH = pl.DeviceIdType.MESH
DELTAS = (-2, -1, 1, 2)
LANES = 128
HALO = 4


def split_2(x):
    high = x.astype(BF16)
    return high, (x - high.astype(F32)).astype(BF16)


def interval(
    dims,
    atm, offs, edge, rates, mixing, owners, weights, mask, ocean, forcing_mix,
    result, ocean_new, surface_new,
    ring, step1, coef, offs_v, edge_v, rates_s, mix_v, owners_v, weights_v, mask_v, ocean_v, base_v, fmix_v,
    edge_send, edge_recv, sums_a, sums_b, got_a, got_b, flux_send, flux_recv, back_send, back_recv,
    cols_hot, slot_hot, mix_cols,
    atm_sem, in_sem, edge_sem, lev_send_sem, lev_up_sem, lev_down_sem, sum_sem, flux_sem, back_sem,
):
    n_sec, n_patch, n_lev = dims
    ntr, klev, ncol = atm.shape
    alev = klev * n_lev
    block = ncol // n_lev
    slots = weights.shape[0] // n_patch
    copies = LANES // slots
    wide = ncol + 2 * LANES
    rows = klev + 2 * HALO

    sec, patch, lev = lax.axis_index("sec"), lax.axis_index("patch"), lax.axis_index("lev")
    place = sec * n_patch + patch
    n_place = n_sec * n_patch

    def column_neighbour(step):
        other = lax.rem(place + step + n_place, n_place)
        return lax.div(other, n_patch), lax.rem(other, n_patch)

    left, right = column_neighbour(-1), column_neighbour(1)

    def level_of(step):
        return lax.rem(lev + step + n_lev, n_lev)

    barrier = pltpu.get_barrier_semaphore()

    def greet(where):
        pl.semaphore_signal(barrier, inc=1, device_id=where, device_id_type=MESH)

    for step in (-1, 0, 1):
        for s, p in (left, right):
            greet((s, p, level_of(step)))
    for i in range(1, n_lev):
        greet((sec, patch, level_of(i)))

    def greet_patch(i, carry):
        greet((sec, lax.rem(patch + i, n_patch), lev))
        return carry

    lax.fori_loop(1, n_patch, greet_patch, 0)

    small = [
        (offs, offs_v), (edge, edge_v), (rates, rates_s), (owners, owners_v),
        (mixing, mix_v), (forcing_mix, fmix_v), (mask, mask_v), (ocean, ocean_v), (weights, weights_v),
    ]
    loads = [pltpu.make_async_copy(a, b, in_sem.at[i]) for i, (a, b) in enumerate(small)]
    for i in (0, 1):
        loads[i].start()
    atm_loads = [
        pltpu.make_async_copy(atm.at[t], ring.at[t, 0:klev, LANES : LANES + ncol], atm_sem.at[t])
        for t in range(ntr)
    ]
    for load in atm_loads:
        load.start()
    for load in loads[2:]:
        load.start()

    loads[0].wait()
    loads[1].wait()
    offsets, exchange = offs_v[...], edge_v[...]
    total = jnp.zeros((1, ncol), F32)
    for i, delta in enumerate(DELTAS):
        part = jnp.sum(jnp.where(offsets == delta, exchange, 0.0), axis=0, keepdims=True)
        total = total + part
        coef[i, :, LANES : LANES + ncol] = jnp.broadcast_to(part, (8, ncol))
    coef[4, :, LANES : LANES + ncol] = jnp.broadcast_to(1.0 - total, (8, ncol))

    lane = lax.broadcasted_iota(jnp.int32, (8, LANES), 1)
    row = lax.broadcasted_iota(jnp.int32, (8, LANES), 0)
    coef_lane = 2 * ntr * HALO
    for load in atm_loads:
        load.wait()
    first = jnp.zeros((8, LANES), F32)
    last = jnp.zeros((8, LANES), F32)
    for t in range(ntr):
        for k in range(2):
            at = (2 * t + k) * HALO
            here = (lane >= at) & (lane < at + HALO)
            a = ring[t, 8 * k : 8 * k + 8, LANES : 2 * LANES]
            b = ring[t, 8 * k : 8 * k + 8, ncol : ncol + LANES]
            first = jnp.where(here, pltpu.roll(a, at, 1) if at else a, first)
            last = jnp.where(here, pltpu.roll(b, at + HALO, 1), last)
    here = (lane >= coef_lane) & (lane < coef_lane + HALO)
    for i in range(4):
        a = coef[i, :, LANES : 2 * LANES]
        b = coef[i, :, ncol : ncol + LANES]
        first = jnp.where(here & (row == i), pltpu.roll(a, coef_lane, 1), first)
        last = jnp.where(here & (row == i), pltpu.roll(b, coef_lane + HALO, 1), last)
    edge_send[0] = first
    edge_send[1] = last

    pl.semaphore_wait(barrier, 6 + (n_lev - 1) + (n_patch - 1))

    for side, (s, p) in ((0, right), (1, left)):
        for step in (0, -1, 1):
            pltpu.make_async_remote_copy(
                src_ref=edge_send.at[1 - side],
                dst_ref=edge_recv.at[side, 1 - step],
                send_sem=edge_sem.at[0],
                recv_sem=edge_sem.at[1],
                device_id=(s, p, level_of(step)),
                device_id_type=MESH,
            ).start()

    def to_lower(t):
        return pltpu.make_async_remote_copy(
            src_ref=atm.at[t, 0:HALO, :],
            dst_ref=ring.at[t, klev : klev + HALO, LANES : LANES + ncol],
            send_sem=lev_send_sem.at[0, t],
            recv_sem=lev_up_sem.at[t],
            device_id=(sec, patch, level_of(-1)),
            device_id_type=MESH,
        )

    def to_upper(t):
        return pltpu.make_async_remote_copy(
            src_ref=atm.at[t, klev - HALO : klev, :],
            dst_ref=ring.at[t, klev + HALO : rows, LANES : LANES + ncol],
            send_sem=lev_send_sem.at[1, t],
            recv_sem=lev_down_sem.at[t],
            device_id=(sec, patch, level_of(1)),
            device_id_type=MESH,
        )

    @pl.when(lev > 0)
    def _():
        for t in range(ntr):
            to_lower(t).start()

    @pl.when(lev < n_lev - 1)
    def _():
        for t in range(ntr):
            to_upper(t).start()

    @pl.when(lev == 0)
    def _():
        ring[:, klev + HALO : rows, LANES : LANES + ncol] = jnp.zeros((ntr, HALO, ncol), F32)

    @pl.when(lev == n_lev - 1)
    def _():
        ring[:, klev : klev + HALO, LANES : LANES + ncol] = jnp.zeros((ntr, HALO, ncol), F32)

    for load in loads[2:]:
        load.wait()
    owned = owners_v[...]
    hot = (lax.broadcasted_iota(jnp.int32, (n_patch, block), 0) == owned).astype(F32)
    cols_hot[...] = hot
    earlier = (
        lax.broadcasted_iota(jnp.int32, (block, block), 0) < lax.broadcasted_iota(jnp.int32, (block, block), 1)
    ).astype(F32).astype(BF16)
    rank = jnp.dot(hot.astype(BF16), earlier, preferred_element_type=F32)
    slot = jnp.sum(rank * hot, axis=0, keepdims=True).astype(jnp.int32)
    lane_slot = lax.rem(lax.broadcasted_iota(jnp.int32, (LANES, block), 0), slots)
    slot_hot[...] = (lane_slot == slot).astype(F32).astype(BF16)
    for t in range(ntr):
        mix_cols[t] = jnp.broadcast_to(mix_v[:, t : t + 1], (mixing.shape[0], block))

    state = ocean_v[...]
    nol = state.shape[1]
    level = lax.broadcasted_iota(jnp.int32, state.shape, 1)
    above = jnp.where(level < nol - 1, pltpu.roll(state, nol - 1, 1) - state, 0.0)
    below = jnp.where(level > 0, pltpu.roll(state, 1, 1) - state, 0.0)
    base_v[...] = state + 0.2 * above + 0.2 * below

    ring_row = lax.broadcasted_iota(jnp.int32, (rows, LANES), 0)
    k = lev * klev + jnp.where(ring_row < klev + HALO, ring_row, ring_row - rows)
    inside = (k >= 0) & (k < alev)
    vertical = (
        3.0
        - (k < 1).astype(F32) - 0.5 * (k < 2).astype(F32)
        - (k > alev - 2).astype(F32) - 0.5 * (k > alev - 3).astype(F32)
    )
    inside_halo = inside[klev:, :]

    def across(x, times):
        return jnp.concatenate([x] * times, axis=1) if times > 1 else x

    def down(x):
        return jnp.concatenate([x] * (rows // 8), axis=0)

    def stencil(x, at, tiles, rate, rate_vertical):
        width = tiles * LANES
        middle = x[:, LANES : LANES + width]
        out = middle * (down(coef[4, :, at : at + width]) - across(rate_vertical, tiles))
        for i, delta in enumerate(DELTAS):
            moved = pltpu.roll(x, (-delta) % x.shape[1], 1)[:, LANES : LANES + width]
            out = out + down(coef[i, :, at : at + width]) * moved
        one = pltpu.roll(middle, 1, 0) + pltpu.roll(middle, rows - 1, 0)
        two = pltpu.roll(middle, 2, 0) + pltpu.roll(middle, rows - 2, 0)
        return out + rate * (one + 0.5 * two)

    def masked(x, tiles):
        return jnp.concatenate(
            [x[:klev], jnp.where(across(inside_halo, tiles), x[klev:], 0.0)], axis=0
        )

    n_tiles = ncol // LANES
    per_block = block // LANES
    n_a = sums_a.shape[2]

    def step_1(t, first, tiles, rate, rate_vertical):
        at = LANES * (1 + first)
        x = ring[t, :, at - LANES : at + (tiles + 1) * LANES]
        step1[t, :, at : at + tiles * LANES] = masked(stencil(x, at, tiles, rate, rate_vertical), tiles)

    def step_2(t, first, tiles, rate, rate_vertical, sums, at_row):
        at = LANES * (1 + first)
        x = step1[t, :, at - LANES : at + (tiles + 1) * LANES]
        out = stencil(x, at, tiles, rate, rate_vertical)[:klev]
        result[t, :, at - LANES : at + (tiles - 1) * LANES] = out
        column_sums = jnp.sum(out, axis=0, keepdims=True)
        for i in range(tiles):
            d, half = divmod(first + i, per_block)
            sums[d, half, pl.ds(at_row, 1), :] = column_sums[:, i * LANES : (i + 1) * LANES]

    def inner(t, sums, at_row):
        @pl.when(lev < n_lev - 1)
        def _():
            to_lower(t).wait_recv()

        @pl.when(lev > 0)
        def _():
            to_upper(t).wait_recv()

        rate = rates_s[t]
        rate_vertical = rate * vertical
        for first in range(0, n_tiles, 4):
            step_1(t, first, 4, rate, rate_vertical)
        for first in range(0, n_tiles, 4):
            low, high = max(first, 1), min(first + 4, n_tiles - 1)
            step_2(t, low, high - low, rate, rate_vertical, sums, at_row)

    def outer(t, sums, at_row):
        rate = rates_s[t]
        rate_vertical = rate * vertical
        low, high = 2 * HALO * t, 2 * HALO * t + HALO

        def sides(from_left, from_right, lanes_at):
            return jnp.where(
                lane < LANES // 2,
                pltpu.roll(from_right, lax.rem(LANES - lanes_at, LANES), 1),
                pltpu.roll(from_left, LANES - HALO - lanes_at, 1),
            )

        corner = jnp.where(
            row < HALO,
            sides(edge_recv[0, 2], edge_recv[1, 2], low),
            sides(edge_recv[0, 0], edge_recv[1, 0], high),
        )
        halo = jnp.concatenate(
            [
                sides(edge_recv[0, 1], edge_recv[1, 1], low),
                sides(edge_recv[0, 1], edge_recv[1, 1], high),
                jnp.where(inside_halo, corner, 0.0),
            ],
            axis=0,
        )
        ring[t, :, 0:LANES] = halo
        ring[t, :, LANES + ncol : wide] = halo

        x = jnp.concatenate([ring[t, :, ncol : ncol + LANES], halo, ring[t, :, LANES : 2 * LANES]], axis=1)
        halo = masked(stencil(x, 0, 1, rate, rate_vertical), 1)
        step1[t, :, 0:LANES] = halo
        step1[t, :, LANES + ncol : wide] = halo
        for first in (0, n_tiles - 1):
            step_1(t, first, 1, rate, rate_vertical)
            step_2(t, first, 1, rate, rate_vertical, sums, at_row)

    def send_sums(sums, got, which, levels):
        for d in levels:
            @pl.when(lev != d)
            def _(d=d):
                pltpu.make_async_remote_copy(
                    src_ref=sums.at[d],
                    dst_ref=got.at[lax.rem(lev - d + n_lev, n_lev) - 1],
                    send_sem=sum_sem.at[0, which],
                    recv_sem=sum_sem.at[1, which],
                    device_id=(sec, patch, d),
                    device_id_type=MESH,
                ).start()

    def all_tracers(step):
        def with_a(t, carry):
            step(t, sums_a, t)
            return carry

        def with_b(t, carry):
            step(t, sums_b, t - n_a)
            return carry

        lax.fori_loop(0, n_a, with_a, 0)
        lax.fori_loop(n_a, ntr, with_b, 0)

    all_tracers(inner)
    for sums, got, which in ((sums_a, got_a, 0), (sums_b, got_b, 1)):
        send_sums(sums, got, which, range(1, n_lev - 1))

    pltpu.make_async_copy(edge_recv, edge_recv, edge_sem.at[1]).wait()
    beside = jnp.where(
        lane < LANES // 2,
        pltpu.roll(edge_recv[1, 1], LANES - coef_lane, 1),
        pltpu.roll(edge_recv[0, 1], LANES - HALO - coef_lane, 1),
    )
    total = jnp.zeros((1, LANES), F32)
    for i in range(4):
        part = beside[i : i + 1, :]
        total = total + part
        for at in (0, LANES + ncol):
            coef[i, :, at : at + LANES] = jnp.broadcast_to(part, (8, LANES))
    for at in (0, LANES + ncol):
        coef[4, :, at : at + LANES] = jnp.broadcast_to(1.0 - total, (8, LANES))

    all_tracers(outer)
    for sums, got, which in ((sums_a, got_a, 0), (sums_b, got_b, 1)):
        send_sums(sums, got, which, (0, n_lev - 1))

    pick = (
        lax.broadcasted_iota(jnp.int32, (ntr, ntr), 0) == lax.broadcasted_iota(jnp.int32, (ntr, ntr), 1)
    )
    fmix = fmix_v[...]
    fmix_cols = [
        jnp.sum(jnp.where(pick, jnp.broadcast_to(fmix[v : v + 1, :], (ntr, ntr)), 0.0), axis=1, keepdims=True)
        for v in range(2)
    ]

    def level_sums(sums, got, which):
        pltpu.make_async_copy(got, got, sum_sem.at[1, which]).wait()
        out = sums[lev]
        for i in range(n_lev - 1):
            out = out + got[i]
        return jnp.concatenate([out[i] for i in range(per_block)], axis=1)

    mean_a = level_sums(sums_a, got_a, 0) * (1.0 / alev)
    mixed = jnp.zeros((mixing.shape[0], block), F32)
    for t in range(n_a):
        mixed = mixed + mix_cols[t] * mean_a[t : t + 1, :]
    mean_b = level_sums(sums_b, got_b, 1) * (1.0 / alev)
    for t in range(n_a, ntr):
        mixed = mixed + mix_cols[t] * mean_b[t - n_a : t - n_a + 1, :]
    flux = jnp.tanh(mixed)
    hot = cols_hot[...]
    parts = []
    for v in range(2):
        forced = jnp.sum(fmix_cols[v] * flux, axis=0, keepdims=True)
        parts += [(hot * piece.astype(F32)).astype(BF16) for piece in split_2(forced)]
    slot_map = slot_hot[...]
    out = lax.dot_general(
        jnp.concatenate(parts, axis=0), slot_map, (((1,), (1,)), ((), ())), preferred_element_type=F32
    )
    outgoing = [out[2 * v * n_patch : (2 * v + 1) * n_patch] + out[(2 * v + 1) * n_patch : (2 * v + 2) * n_patch] for v in range(2)]
    for v in range(2):
        flux_send[:, v * LANES : (v + 1) * LANES] = outgoing[v]

    def send_flux(i, carry):
        other = lax.rem(patch + i, n_patch)
        pltpu.make_async_remote_copy(
            src_ref=flux_send.at[pl.ds(other, 1), :],
            dst_ref=flux_recv.at[pl.ds(patch, 1), :],
            send_sem=flux_sem.at[0],
            recv_sem=flux_sem.at[1],
            device_id=(sec, other, lev),
            device_id_type=MESH,
        ).start()
        return carry

    lax.fori_loop(1, n_patch, send_flux, 0)
    own_row = pl.ds(patch, 1)
    pltpu.make_async_copy(flux_send.at[own_row, :], flux_recv.at[own_row, :], flux_sem.at[1]).start()
    ocean_cells = mask_v[...].astype(F32)
    pltpu.make_async_copy(flux_recv, flux_recv, flux_sem.at[1]).wait()

    groups = n_patch * slots // LANES
    received = []
    for v in range(2):
        pieces = []
        for g in range(groups):
            tile = flux_recv[g * copies : (g + 1) * copies, v * LANES : (v + 1) * LANES]
            pieces.append(jnp.sum(jnp.where(lax.div(lane, slots) == row, tile, 0.0), axis=0, keepdims=True))
        received.append(jnp.concatenate(pieces, axis=1))
    w = weights_v[...]

    def stacked(values):
        at = lax.broadcasted_iota(jnp.int32, (16, values[0].shape[1]), 0)
        out = jnp.zeros((16, values[0].shape[1]), F32)
        for i, value in enumerate(values):
            out = jnp.where(at == i, value.astype(F32), out)
        return out.astype(BF16)

    sums = jnp.dot(stacked([*split_2(received[0]), *split_2(received[1])]), w, preferred_element_type=F32)
    forcing = [(sums[2 * v : 2 * v + 1] + sums[2 * v + 1 : 2 * v + 2]) * ocean_cells for v in range(2)]
    warmth = (base_v[0, 0:1, :] + forcing[0]) * ocean_cells
    back = lax.dot_general(
        stacked([*split_2(warmth)]), w, (((1,), (1,)), ((), ())), preferred_element_type=F32
    )
    back = back[0:1] + back[1:2]
    for g in range(groups):
        back_send[g : g + 1, :] = back[:, g * LANES : (g + 1) * LANES]

    def send_back(i, carry):
        other = lax.rem(patch + i, n_patch)
        pltpu.make_async_remote_copy(
            src_ref=back_send.at[pl.ds(lax.div(other, copies), 1), :],
            dst_ref=back_recv.at[pl.ds(patch, 1), :],
            send_sem=back_sem.at[0],
            recv_sem=back_sem.at[1],
            device_id=(sec, other, lev),
            device_id_type=MESH,
        ).start()
        return carry

    lax.fori_loop(1, n_patch, send_back, 0)
    pltpu.make_async_copy(
        back_send.at[pl.ds(lax.div(patch, copies), 1), :], back_recv.at[own_row, :], back_sem.at[1]
    ).start()

    depth = lax.broadcasted_iota(jnp.int32, (nol, block), 0).astype(F32)
    profile = jnp.exp(-depth / 8.0)
    for v in range(2):
        ocean_new[v] = base_v[v] + profile * forcing[v]

    pltpu.make_async_copy(back_recv, back_recv, back_sem.at[1]).wait()
    at_lane = lax.broadcasted_iota(jnp.int32, (n_patch, LANES), 1)
    own = lax.div(at_lane, slots) == lax.rem(patch, copies)
    returned = jnp.where(own, back_recv[...], 0.0)
    values = jnp.dot(jnp.concatenate(split_2(returned), axis=0), slot_map, preferred_element_type=F32)
    surface_new[...] = jnp.sum((values[:n_patch] + values[n_patch:]) * hot, axis=0, keepdims=True)

    six = edge_recv
    pltpu.make_async_copy(six, six, edge_sem.at[0]).wait()

    @pl.when(lev > 0)
    def _():
        for t in range(ntr):
            to_lower(t).wait_send()

    @pl.when(lev < n_lev - 1)
    def _():
        for t in range(ntr):
            to_upper(t).wait_send()

    pltpu.make_async_copy(got_a, got_a, sum_sem.at[0, 0]).wait()
    pltpu.make_async_copy(got_b, got_b, sum_sem.at[0, 1]).wait()
    count = n_patch // 2
    while count:
        for ref, sem in ((flux_recv, flux_sem), (back_recv, back_sem)):
            some = ref.at[pl.ds(0, count), :]
            pltpu.make_async_copy(some, some, sem.at[0]).wait()
        count //= 2


def store(a, b, c, a_out, b_out, c_out, sem):
    copies = [pltpu.make_async_copy(x, y, sem.at[i]) for i, (x, y) in enumerate(((a, a_out), (b, b_out), (c, c_out)))]
    for copy in copies:
        copy.start()
    for copy in copies:
        copy.wait()


def solution(mesh):
    dims = tuple(mesh.shape[a] for a in ("sec", "patch", "lev"))
    n_sec, n_patch, n_lev = dims

    def per_device(atm, offs, edge, rates, mixing, owners, weights, mask, ocean, forcing_mix):
        ntr, klev, ncol = atm.shape
        rows, wide = klev + 2 * HALO, ncol + 2 * LANES
        block = ncol // n_lev
        nflux = mixing.shape[0]
        owners, mask = owners.reshape(1, -1), mask.reshape(1, -1)
        dma = pltpu.SemaphoreType.DMA
        vmem = pltpu.VMEM
        any_space = pl.BlockSpec(memory_space=pltpu.HBM)
        in_vmem = pl.BlockSpec(memory_space=pltpu.VMEM)
        operands = [
            pltpu.with_memory_space_constraint(x, pltpu.HBM)
            for x in (atm, offs, edge, rates, mixing, owners, weights, mask, ocean, forcing_mix)
        ]
        out = pl.pallas_call(
            functools.partial(interval, dims),
            out_shape=(
                jax.ShapeDtypeStruct(atm.shape, F32),
                jax.ShapeDtypeStruct(ocean.shape, F32),
                jax.ShapeDtypeStruct((1, block), F32),
            ),
            in_specs=[any_space] * 10,
            out_specs=(in_vmem,) * 3,
            scratch_shapes=[
                vmem((ntr, rows, wide), F32),
                vmem((ntr, rows, wide), F32),
                vmem((5, 8, wide), F32),
                vmem(offs.shape, jnp.int32),
                vmem(edge.shape, F32),
                pltpu.SMEM(rates.shape, F32),
                vmem(mixing.shape, F32),
                vmem(owners.shape, jnp.int32),
                vmem(weights.shape, BF16),
                vmem(mask.shape, jnp.int32),
                vmem(ocean.shape, F32),
                vmem(ocean.shape, F32),
                vmem(forcing_mix.shape, F32),
                vmem((2, 8, LANES), F32),
                vmem((2, 3, 8, LANES), F32),
                vmem((n_lev, block // LANES, 8, LANES), F32),
                vmem((n_lev, block // LANES, ntr - 8, LANES), F32),
                vmem((n_lev - 1, block // LANES, 8, LANES), F32),
                vmem((n_lev - 1, block // LANES, ntr - 8, LANES), F32),
                vmem((n_patch, 2 * LANES), F32),
                vmem((n_patch, 2 * LANES), F32),
                vmem((weights.shape[0] // LANES, LANES), F32),
                vmem((n_patch, LANES), F32),
                vmem((n_patch, block), F32),
                vmem((LANES, block), BF16),
                vmem((ntr, nflux, block), F32),
                dma((ntr,)),
                dma((9,)),
                dma((2,)),
                dma((2, ntr)),
                dma((ntr,)),
                dma((ntr,)),
                dma((2, 2)),
                dma((2,)),
                dma((2,)),
            ],
            compiler_params=pltpu.CompilerParams(
                collective_id=0, has_side_effects=True, vmem_limit_bytes=40 * 1024 * 1024
            ),
            name="interval",
        )(*operands)
        out = pl.pallas_call(
            store,
            out_shape=tuple(jax.ShapeDtypeStruct(x.shape, F32) for x in out),
            in_specs=[in_vmem] * 3,
            out_specs=(any_space,) * 3,
            scratch_shapes=[dma((3,))],
            name="store",
        )(*out)
        return out[0], out[1], out[2].reshape(-1)

    in_specs = (
        P(None, "lev", ("sec", "patch")),
        P(None, ("sec", "patch")),
        P(None, ("sec", "patch")),
        P(),
        P(),
        P(("sec", "patch", "lev"), None),
        P(None, ("sec", "patch", "lev")),
        P(("sec", "patch", "lev")),
        P(None, None, ("sec", "patch", "lev")),
        P(),
    )
    out_specs = (
        P(None, "lev", ("sec", "patch")),
        P(None, None, ("sec", "patch", "lev")),
        P(("sec", "patch", "lev")),
    )
    return jax.shard_map(per_device, mesh=mesh, in_specs=in_specs, out_specs=out_specs, check_vma=False)
```

```python
import functools
import jax
import jax.numpy as jnp
from jax import lax
from jax.experimental import pallas as pl
from jax.experimental.pallas import tpu as pltpu
from jax.sharding import PartitionSpec as P

F32 = jnp.float32
BF16 = jnp.bfloat16
MESH = pl.DeviceIdType.MESH
DELTAS = (-2, -1, 1, 2)
LANES = 128
HALO = 4


def split_2(x):
    high = x.astype(BF16)
    return high, (x - high.astype(F32)).astype(BF16)


def interval(
    dims,
    atm, offs, edge, rates, mixing, owners, weights, mask, ocean, forcing_mix,
    result, ocean_new, surface_new,
    ring, step1, coef, offs_v, edge_v, rates_s, mix_v, owners_v, weights_v, mask_v, ocean_v, base_v, fmix_v,
    edge_send, edge_recv, sums_a, sums_b, got_a, got_b, flux_send, flux_recv, back_send, back_recv,
    cols_hot, slot_hot, mix_cols,
    atm_sem, in_sem, edge_sem, lev_send_sem, lev_up_sem, lev_down_sem, sum_sem, flux_sem, back_sem,
):
    n_sec, n_patch, n_lev = dims
    ntr, klev, ncol = atm.shape
    alev = klev * n_lev
    block = ncol // n_lev
    slots = weights.shape[0] // n_patch
    copies = LANES // slots
    wide = ncol + 2 * LANES
    rows = klev + 2 * HALO

    sec, patch, lev = lax.axis_index("sec"), lax.axis_index("patch"), lax.axis_index("lev")
    place = sec * n_patch + patch
    n_place = n_sec * n_patch

    def column_neighbour(step):
        other = lax.rem(place + step + n_place, n_place)
        return lax.div(other, n_patch), lax.rem(other, n_patch)

    def beside(side):
        s, p = column_neighbour(2 * side - 1)
        return s, p, s < sec, s > sec

    def level_of(step):
        return lax.rem(lev + step + n_lev, n_lev)

    barrier = pltpu.get_barrier_semaphore()

    def greet(where):
        pl.semaphore_signal(barrier, inc=1, device_id=where, device_id_type=MESH)

    expected = (n_lev - 1) + (n_patch - 1)
    for side in range(2):
        s, p, lower, higher = beside(side)

        @pl.when(jnp.logical_not(lower))
        def _(s=s, p=p):
            for step in (-1, 0, 1):
                greet((s, p, level_of(step)))

        expected = expected + jnp.where(higher, 0, 3)
    for i in range(1, n_lev):
        greet((sec, patch, level_of(i)))

    def greet_patch(i, carry):
        greet((sec, lax.rem(patch + i, n_patch), lev))
        return carry

    lax.fori_loop(1, n_patch, greet_patch, 0)

    small = [
        (offs, offs_v), (edge, edge_v), (rates, rates_s), (owners, owners_v),
        (mixing, mix_v), (forcing_mix, fmix_v), (mask, mask_v), (ocean, ocean_v), (weights, weights_v),
    ]
    loads = [pltpu.make_async_copy(a, b, in_sem.at[i]) for i, (a, b) in enumerate(small)]
    for i in (0, 1):
        loads[i].start()
    atm_loads = [
        pltpu.make_async_copy(atm.at[t], ring.at[t, 0:klev, LANES : LANES + ncol], atm_sem.at[t])
        for t in range(ntr)
    ]
    for load in atm_loads:
        load.start()
    for load in loads[2:]:
        load.start()

    loads[0].wait()
    loads[1].wait()
    offsets, exchange = offs_v[...], edge_v[...]
    total = jnp.zeros((1, ncol), F32)
    for i, delta in enumerate(DELTAS):
        part = jnp.sum(jnp.where(offsets == delta, exchange, 0.0), axis=0, keepdims=True)
        total = total + part
        coef[i, :, LANES : LANES + ncol] = jnp.broadcast_to(part, (8, ncol))
    coef[4, :, LANES : LANES + ncol] = jnp.broadcast_to(1.0 - total, (8, ncol))

    lane = lax.broadcasted_iota(jnp.int32, (8, LANES), 1)
    row = lax.broadcasted_iota(jnp.int32, (8, LANES), 0)
    coef_lane = 2 * ntr * HALO
    for load in atm_loads:
        load.wait()
    first = jnp.zeros((8, LANES), F32)
    last = jnp.zeros((8, LANES), F32)
    for t in range(ntr):
        for k in range(2):
            at = (2 * t + k) * HALO
            here = (lane >= at) & (lane < at + HALO)
            a = ring[t, 8 * k : 8 * k + 8, LANES : 2 * LANES]
            b = ring[t, 8 * k : 8 * k + 8, ncol : ncol + LANES]
            first = jnp.where(here, pltpu.roll(a, at, 1) if at else a, first)
            last = jnp.where(here, pltpu.roll(b, at + HALO, 1), last)
    here = (lane >= coef_lane) & (lane < coef_lane + HALO)
    for i in range(4):
        a = coef[i, :, LANES : 2 * LANES]
        b = coef[i, :, ncol : ncol + LANES]
        first = jnp.where(here & (row == i), pltpu.roll(a, coef_lane, 1), first)
        last = jnp.where(here & (row == i), pltpu.roll(b, coef_lane + HALO, 1), last)
    edge_send[0] = first
    edge_send[1] = last

    pl.semaphore_wait(barrier, expected)

    def send_edge(side):
        s, p, _, _ = beside(side)
        for step in (0, -1, 1):
            pltpu.make_async_remote_copy(
                src_ref=edge_send.at[side],
                dst_ref=edge_recv.at[1 - side, 1 - step],
                send_sem=edge_sem.at[0],
                recv_sem=edge_sem.at[2 - side],
                device_id=(s, p, level_of(step)),
                device_id_type=MESH,
            ).start()

    for side in range(2):
        @pl.when(jnp.logical_not(beside(side)[3]))
        def _(side=side):
            send_edge(side)

    def to_lower(t):
        return pltpu.make_async_remote_copy(
            src_ref=atm.at[t, 0:HALO, :],
            dst_ref=ring.at[t, klev : klev + HALO, LANES : LANES + ncol],
            send_sem=lev_send_sem.at[0, t],
            recv_sem=lev_up_sem.at[t],
            device_id=(sec, patch, level_of(-1)),
            device_id_type=MESH,
        )

    def to_upper(t):
        return pltpu.make_async_remote_copy(
            src_ref=atm.at[t, klev - HALO : klev, :],
            dst_ref=ring.at[t, klev + HALO : rows, LANES : LANES + ncol],
            send_sem=lev_send_sem.at[1, t],
            recv_sem=lev_down_sem.at[t],
            device_id=(sec, patch, level_of(1)),
            device_id_type=MESH,
        )

    @pl.when(lev > 0)
    def _():
        for t in range(ntr):
            to_lower(t).start()

    @pl.when(lev < n_lev - 1)
    def _():
        for t in range(ntr):
            to_upper(t).start()

    @pl.when(lev == 0)
    def _():
        ring[:, klev + HALO : rows, LANES : LANES + ncol] = jnp.zeros((ntr, HALO, ncol), F32)

    @pl.when(lev == n_lev - 1)
    def _():
        ring[:, klev : klev + HALO, LANES : LANES + ncol] = jnp.zeros((ntr, HALO, ncol), F32)

    for load in loads[2:]:
        load.wait()
    owned = owners_v[...]
    hot = (lax.broadcasted_iota(jnp.int32, (n_patch, block), 0) == owned).astype(F32)
    cols_hot[...] = hot
    earlier = (
        lax.broadcasted_iota(jnp.int32, (block, block), 0) < lax.broadcasted_iota(jnp.int32, (block, block), 1)
    ).astype(F32).astype(BF16)
    rank = jnp.dot(hot.astype(BF16), earlier, preferred_element_type=F32)
    slot = jnp.sum(rank * hot, axis=0, keepdims=True).astype(jnp.int32)
    lane_slot = lax.rem(lax.broadcasted_iota(jnp.int32, (LANES, block), 0), slots)
    slot_hot[...] = (lane_slot == slot).astype(F32).astype(BF16)
    for t in range(ntr):
        mix_cols[t] = jnp.broadcast_to(mix_v[:, t : t + 1], (mixing.shape[0], block))

    state = ocean_v[...]
    nol = state.shape[1]
    level = lax.broadcasted_iota(jnp.int32, state.shape, 1)
    above = jnp.where(level < nol - 1, pltpu.roll(state, nol - 1, 1) - state, 0.0)
    below = jnp.where(level > 0, pltpu.roll(state, 1, 1) - state, 0.0)
    base_v[...] = state + 0.2 * above + 0.2 * below

    ring_row = lax.broadcasted_iota(jnp.int32, (rows, LANES), 0)
    k = lev * klev + jnp.where(ring_row < klev + HALO, ring_row, ring_row - rows)
    inside = (k >= 0) & (k < alev)
    vertical = (
        3.0
        - (k < 1).astype(F32) - 0.5 * (k < 2).astype(F32)
        - (k > alev - 2).astype(F32) - 0.5 * (k > alev - 3).astype(F32)
    )
    inside_halo = inside[klev:, :]

    def halo_lane(side):
        return (1 - side) * (LANES - HALO)

    def halo_at(side):
        return pl.multiple_of(side * (LANES + ncol), LANES)

    def across(x, times):
        return jnp.concatenate([x] * times, axis=1) if times > 1 else x

    def down(x):
        return jnp.concatenate([x] * (rows // 8), axis=0)

    def stencil(x, at, first, tiles, rate, rate_vertical):
        width = tiles * LANES
        part = slice(first * LANES, first * LANES + width)
        middle = x[:, part]
        columns = pl.ds(at, width)
        out = middle * (down(coef[4, :, columns]) - across(rate_vertical, tiles))
        for i, delta in enumerate(DELTAS):
            moved = pltpu.roll(x, (-delta) % x.shape[1], 1)[:, part]
            out = out + down(coef[i, :, columns]) * moved
        one = pltpu.roll(middle, 1, 0) + pltpu.roll(middle, rows - 1, 0)
        two = pltpu.roll(middle, 2, 0) + pltpu.roll(middle, rows - 2, 0)
        return out + rate * (one + 0.5 * two)

    def masked(x, tiles):
        return jnp.concatenate(
            [x[:klev], jnp.where(across(inside_halo, tiles), x[klev:], 0.0)], axis=0
        )

    n_tiles = ncol // LANES
    per_block = block // LANES
    n_a = sums_a.shape[2]

    def step_1(t, first, tiles, rate, rate_vertical):
        at = LANES * (1 + first)
        x = ring[t, :, at - LANES : at + (tiles + 1) * LANES]
        step1[:, at : at + tiles * LANES] = masked(stencil(x, at, 1, tiles, rate, rate_vertical), tiles)

    def step_2(t, first, tiles, rate, rate_vertical, sums, at_row):
        at = LANES * (1 + first)
        x = step1[:, at - LANES : at + (tiles + 1) * LANES]
        out = stencil(x, at, 1, tiles, rate, rate_vertical)[:klev]
        result[t, :, at - LANES : at + (tiles - 1) * LANES] = out
        column_sums = jnp.sum(out, axis=0, keepdims=True)
        for i in range(tiles):
            d, half = divmod(first + i, per_block)
            sums[d, half, pl.ds(at_row, 1), :] = column_sums[:, i * LANES : (i + 1) * LANES]

    def inner(t, sums, at_row):
        @pl.when(lev < n_lev - 1)
        def _():
            to_lower(t).wait_recv()

        @pl.when(lev > 0)
        def _():
            to_upper(t).wait_recv()

        rate = rates_s[t]
        rate_vertical = rate * vertical
        for first in range(0, n_tiles, 4):
            step_1(t, first, 4, rate, rate_vertical)
        for first in range(0, n_tiles, 4):
            low, high = max(first, 1), min(first + 4, n_tiles - 1)
            step_2(t, low, high - low, rate, rate_vertical, sums, at_row)

    def outer(side, t, sums, at_row):
        rate = rates_s[t]
        rate_vertical = rate * vertical
        low, high = 2 * HALO * t, 2 * HALO * t + HALO

        def moved(level, lanes_at):
            return pltpu.roll(edge_recv[side, level], lax.rem(halo_lane(side) - lanes_at + LANES, LANES), 1)

        halo = jnp.concatenate(
            [
                moved(1, low),
                moved(1, high),
                jnp.where(inside_halo, jnp.where(row < HALO, moved(2, low), moved(0, high)), 0.0),
            ],
            axis=0,
        )
        ring[t, :, pl.ds(halo_at(side), LANES)] = halo
        start = pl.multiple_of(side * (wide - 3 * LANES), LANES)
        x = ring[t, :, pl.ds(start, 3 * LANES)]
        x = masked(stencil(x, start, 0, 3, rate, rate_vertical), 3)
        out = stencil(x, pl.multiple_of(start + LANES, LANES), 1, 1, rate, rate_vertical)[:klev]
        result[t, :, pl.ds(pl.multiple_of(side * (ncol - LANES), LANES), LANES)] = out
        sums[side * (n_lev - 1), side * (per_block - 1), pl.ds(at_row, 1), :] = jnp.sum(out, axis=0, keepdims=True)

    def send_sums(d):
        @pl.when(lev != d)
        def _():
            for which, (sums, got) in enumerate(((sums_a, got_a), (sums_b, got_b))):
                pltpu.make_async_remote_copy(
                    src_ref=sums.at[d],
                    dst_ref=got.at[lax.rem(lev - d + n_lev, n_lev) - 1],
                    send_sem=sum_sem.at[0, which],
                    recv_sem=sum_sem.at[1, which],
                    device_id=(sec, patch, d),
                    device_id_type=MESH,
                ).start()

    def all_tracers(step):
        def with_a(t, carry):
            step(t, sums_a, t)
            return carry

        def with_b(t, carry):
            step(t, sums_b, t - n_a)
            return carry

        lax.fori_loop(0, n_a, with_a, 0)
        lax.fori_loop(n_a, ntr, with_b, 0)

    all_tracers(inner)
    for d in range(1, n_lev - 1):
        send_sums(d)

    def one_side(i, carry):
        side = lax.rem(i + (patch == 0).astype(jnp.int32), 2)
        here = edge_recv.at[side]
        pltpu.make_async_copy(here, here, edge_sem.at[1 + side]).wait()

        @pl.when(beside(side)[3])
        def _():
            send_edge(side)

        around = pltpu.roll(edge_recv[side, 1], lax.rem(halo_lane(side) - coef_lane + LANES, LANES), 1)
        total = jnp.zeros((1, LANES), F32)
        columns = pl.ds(halo_at(side), LANES)
        for k in range(4):
            part = around[k : k + 1, :]
            total = total + part
            coef[k, :, columns] = jnp.broadcast_to(part, (8, LANES))
        coef[4, :, columns] = jnp.broadcast_to(1.0 - total, (8, LANES))
        all_tracers(functools.partial(outer, side))
        send_sums(side * (n_lev - 1))
        return carry

    lax.fori_loop(0, 2, one_side, 0)

    pick = (
        lax.broadcasted_iota(jnp.int32, (ntr, ntr), 0) == lax.broadcasted_iota(jnp.int32, (ntr, ntr), 1)
    )
    fmix = fmix_v[...]
    fmix_cols = [
        jnp.sum(jnp.where(pick, jnp.broadcast_to(fmix[v : v + 1, :], (ntr, ntr)), 0.0), axis=1, keepdims=True)
        for v in range(2)
    ]

    def level_sums(sums, got, which):
        pltpu.make_async_copy(got, got, sum_sem.at[1, which]).wait()
        out = sums[lev]
        for i in range(n_lev - 1):
            out = out + got[i]
        return jnp.concatenate([out[i] for i in range(per_block)], axis=1)

    mean_a = level_sums(sums_a, got_a, 0) * (1.0 / alev)
    mixed = jnp.zeros((mixing.shape[0], block), F32)
    for t in range(n_a):
        mixed = mixed + mix_cols[t] * mean_a[t : t + 1, :]
    mean_b = level_sums(sums_b, got_b, 1) * (1.0 / alev)
    for t in range(n_a, ntr):
        mixed = mixed + mix_cols[t] * mean_b[t - n_a : t - n_a + 1, :]
    flux = jnp.tanh(mixed)
    hot = cols_hot[...]
    parts = []
    for v in range(2):
        forced = jnp.sum(fmix_cols[v] * flux, axis=0, keepdims=True)
        parts += [(hot * piece.astype(F32)).astype(BF16) for piece in split_2(forced)]
    slot_map = slot_hot[...]
    out = lax.dot_general(
        jnp.concatenate(parts, axis=0), slot_map, (((1,), (1,)), ((), ())), preferred_element_type=F32
    )
    outgoing = [out[2 * v * n_patch : (2 * v + 1) * n_patch] + out[(2 * v + 1) * n_patch : (2 * v + 2) * n_patch] for v in range(2)]
    for v in range(2):
        flux_send[:, v * LANES : (v + 1) * LANES] = outgoing[v]

    def send_flux(i, carry):
        other = lax.rem(patch + i, n_patch)
        pltpu.make_async_remote_copy(
            src_ref=flux_send.at[pl.ds(other, 1), :],
            dst_ref=flux_recv.at[pl.ds(patch, 1), :],
            send_sem=flux_sem.at[0],
            recv_sem=flux_sem.at[1],
            device_id=(sec, other, lev),
            device_id_type=MESH,
        ).start()
        return carry

    lax.fori_loop(1, n_patch, send_flux, 0)
    own_row = pl.ds(patch, 1)
    pltpu.make_async_copy(flux_send.at[own_row, :], flux_recv.at[own_row, :], flux_sem.at[1]).start()
    ocean_cells = mask_v[...].astype(F32)
    pltpu.make_async_copy(flux_recv, flux_recv, flux_sem.at[1]).wait()

    groups = n_patch * slots // LANES
    received = []
    for v in range(2):
        pieces = []
        for g in range(groups):
            tile = flux_recv[g * copies : (g + 1) * copies, v * LANES : (v + 1) * LANES]
            pieces.append(jnp.sum(jnp.where(lax.div(lane, slots) == row, tile, 0.0), axis=0, keepdims=True))
        received.append(jnp.concatenate(pieces, axis=1))
    w = weights_v[...]

    def stacked(values):
        at = lax.broadcasted_iota(jnp.int32, (16, values[0].shape[1]), 0)
        out = jnp.zeros((16, values[0].shape[1]), F32)
        for i, value in enumerate(values):
            out = jnp.where(at == i, value.astype(F32), out)
        return out.astype(BF16)

    sums = jnp.dot(stacked([*split_2(received[0]), *split_2(received[1])]), w, preferred_element_type=F32)
    forcing = [(sums[2 * v : 2 * v + 1] + sums[2 * v + 1 : 2 * v + 2]) * ocean_cells for v in range(2)]
    warmth = (base_v[0, 0:1, :] + forcing[0]) * ocean_cells
    back = lax.dot_general(
        stacked([*split_2(warmth)]), w, (((1,), (1,)), ((), ())), preferred_element_type=F32
    )
    back = back[0:1] + back[1:2]
    for g in range(groups):
        back_send[g : g + 1, :] = back[:, g * LANES : (g + 1) * LANES]

    def send_back(i, carry):
        other = lax.rem(patch + i, n_patch)
        pltpu.make_async_remote_copy(
            src_ref=back_send.at[pl.ds(lax.div(other, copies), 1), :],
            dst_ref=back_recv.at[pl.ds(patch, 1), :],
            send_sem=back_sem.at[0],
            recv_sem=back_sem.at[1],
            device_id=(sec, other, lev),
            device_id_type=MESH,
        ).start()
        return carry

    lax.fori_loop(1, n_patch, send_back, 0)
    pltpu.make_async_copy(
        back_send.at[pl.ds(lax.div(patch, copies), 1), :], back_recv.at[own_row, :], back_sem.at[1]
    ).start()

    depth = lax.broadcasted_iota(jnp.int32, (nol, block), 0).astype(F32)
    profile = jnp.exp(-depth / 8.0)
    for v in range(2):
        ocean_new[v] = base_v[v] + profile * forcing[v]

    pltpu.make_async_copy(back_recv, back_recv, back_sem.at[1]).wait()
    at_lane = lax.broadcasted_iota(jnp.int32, (n_patch, LANES), 1)
    own = lax.div(at_lane, slots) == lax.rem(patch, copies)
    returned = jnp.where(own, back_recv[...], 0.0)
    values = jnp.dot(jnp.concatenate(split_2(returned), axis=0), slot_map, preferred_element_type=F32)
    surface_new[...] = jnp.sum((values[:n_patch] + values[n_patch:]) * hot, axis=0, keepdims=True)

    pltpu.make_async_copy(edge_recv, edge_recv, edge_sem.at[0]).wait()

    @pl.when(lev > 0)
    def _():
        for t in range(ntr):
            to_lower(t).wait_send()

    @pl.when(lev < n_lev - 1)
    def _():
        for t in range(ntr):
            to_upper(t).wait_send()

    pltpu.make_async_copy(got_a, got_a, sum_sem.at[0, 0]).wait()
    pltpu.make_async_copy(got_b, got_b, sum_sem.at[0, 1]).wait()
    count = n_patch // 2
    while count:
        for ref, sem in ((flux_recv, flux_sem), (back_recv, back_sem)):
            some = ref.at[pl.ds(0, count), :]
            pltpu.make_async_copy(some, some, sem.at[0]).wait()
        count //= 2


def store(a, b, c, a_out, b_out, c_out, sem):
    copies = [pltpu.make_async_copy(x, y, sem.at[i]) for i, (x, y) in enumerate(((a, a_out), (b, b_out), (c, c_out)))]
    for copy in copies:
        copy.start()
    for copy in copies:
        copy.wait()


def solution(mesh):
    dims = tuple(mesh.shape[a] for a in ("sec", "patch", "lev"))
    n_sec, n_patch, n_lev = dims

    def per_device(atm, offs, edge, rates, mixing, owners, weights, mask, ocean, forcing_mix):
        ntr, klev, ncol = atm.shape
        rows, wide = klev + 2 * HALO, ncol + 2 * LANES
        block = ncol // n_lev
        nflux = mixing.shape[0]
        owners, mask = owners.reshape(1, -1), mask.reshape(1, -1)
        dma = pltpu.SemaphoreType.DMA
        vmem = pltpu.VMEM
        any_space = pl.BlockSpec(memory_space=pltpu.HBM)
        in_vmem = pl.BlockSpec(memory_space=pltpu.VMEM)
        operands = [
            pltpu.with_memory_space_constraint(x, pltpu.HBM)
            for x in (atm, offs, edge, rates, mixing, owners, weights, mask, ocean, forcing_mix)
        ]
        out = pl.pallas_call(
            functools.partial(interval, dims),
            out_shape=(
                jax.ShapeDtypeStruct(atm.shape, F32),
                jax.ShapeDtypeStruct(ocean.shape, F32),
                jax.ShapeDtypeStruct((1, block), F32),
            ),
            in_specs=[any_space] * 10,
            out_specs=(in_vmem,) * 3,
            scratch_shapes=[
                vmem((ntr, rows, wide), F32),
                vmem((rows, wide), F32),
                vmem((5, 8, wide), F32),
                vmem(offs.shape, jnp.int32),
                vmem(edge.shape, F32),
                pltpu.SMEM(rates.shape, F32),
                vmem(mixing.shape, F32),
                vmem(owners.shape, jnp.int32),
                vmem(weights.shape, BF16),
                vmem(mask.shape, jnp.int32),
                vmem(ocean.shape, F32),
                vmem(ocean.shape, F32),
                vmem(forcing_mix.shape, F32),
                vmem((2, 8, LANES), F32),
                vmem((2, 3, 8, LANES), F32),
                vmem((n_lev, block // LANES, 8, LANES), F32),
                vmem((n_lev, block // LANES, ntr - 8, LANES), F32),
                vmem((n_lev - 1, block // LANES, 8, LANES), F32),
                vmem((n_lev - 1, block // LANES, ntr - 8, LANES), F32),
                vmem((n_patch, 2 * LANES), F32),
                vmem((n_patch, 2 * LANES), F32),
                vmem((weights.shape[0] // LANES, LANES), F32),
                vmem((n_patch, LANES), F32),
                vmem((n_patch, block), F32),
                vmem((LANES, block), BF16),
                vmem((ntr, nflux, block), F32),
                dma((ntr,)),
                dma((9,)),
                dma((3,)),
                dma((2, ntr)),
                dma((ntr,)),
                dma((ntr,)),
                dma((2, 2)),
                dma((2,)),
                dma((2,)),
            ],
            compiler_params=pltpu.CompilerParams(
                collective_id=0, has_side_effects=True, vmem_limit_bytes=40 * 1024 * 1024
            ),
            name="interval",
        )(*operands)
        out = pl.pallas_call(
            store,
            out_shape=tuple(jax.ShapeDtypeStruct(x.shape, F32) for x in out),
            in_specs=[in_vmem] * 3,
            out_specs=(any_space,) * 3,
            scratch_shapes=[dma((3,))],
            compiler_params=pltpu.CompilerParams(vmem_limit_bytes=8 * 1024 * 1024),
            name="store",
        )(*out)
        return out[0], out[1], out[2].reshape(-1)

    in_specs = (
        P(None, "lev", ("sec", "patch")),
        P(None, ("sec", "patch")),
        P(None, ("sec", "patch")),
        P(),
        P(),
        P(("sec", "patch", "lev"), None),
        P(None, ("sec", "patch", "lev")),
        P(("sec", "patch", "lev")),
        P(None, None, ("sec", "patch", "lev")),
        P(),
    )
    out_specs = (
        P(None, "lev", ("sec", "patch")),
        P(None, None, ("sec", "patch", "lev")),
        P(("sec", "patch", "lev")),
    )
    return jax.shard_map(per_device, mesh=mesh, in_specs=in_specs, out_specs=out_specs, check_vma=False)
```

```python
import functools
import jax
import jax.numpy as jnp
from jax import lax
from jax.experimental import pallas as pl
from jax.experimental.pallas import tpu as pltpu
from jax.sharding import PartitionSpec as P

F32 = jnp.float32
BF16 = jnp.bfloat16
MESH = pl.DeviceIdType.MESH
DELTAS = (-2, -1, 1, 2)
LANES = 128
HALO = 4


def split_2(x):
    high = x.astype(BF16)
    return high, (x - high.astype(F32)).astype(BF16)


def interval(
    dims,
    atm, offs, edge, rates, mixing, owners, weights, mask, ocean, forcing_mix,
    result, ocean_new, surface_new,
    ring, step1, coef, offs_v, edge_v, rates_s, mix_v, owners_v, weights_v, mask_v, ocean_v, base_v, fmix_v,
    edge_send, edge_recv, sums_a, sums_b, got_a, got_b, flux_send, flux_recv, back_send, back_recv,
    cols_hot, slot_hot, mix_cols,
    atm_sem, in_sem, edge_sem, answer_sem, lev_send_sem, lev_up_sem, lev_down_sem, sum_sem, flux_sem, back_sem,
):
    n_sec, n_patch, n_lev = dims
    ntr, klev, ncol = atm.shape
    alev = klev * n_lev
    block = ncol // n_lev
    slots = weights.shape[0] // n_patch
    copies = LANES // slots
    wide = ncol + 2 * LANES
    rows = klev + 2 * HALO

    sec, patch, lev = lax.axis_index("sec"), lax.axis_index("patch"), lax.axis_index("lev")
    place = sec * n_patch + patch
    n_place = n_sec * n_patch

    def column_neighbour(step):
        other = lax.rem(place + step + n_place, n_place)
        return lax.div(other, n_patch), lax.rem(other, n_patch)

    def beside(side):
        s, p = column_neighbour(2 * side - 1)
        return s, p, s < sec, s > sec

    def level_of(step):
        return lax.rem(lev + step + n_lev, n_lev)

    barrier = pltpu.get_barrier_semaphore()

    def greet(where):
        pl.semaphore_signal(barrier, inc=1, device_id=where, device_id_type=MESH)

    first_opens = (sec > 0).astype(jnp.int32)
    last_opens = (sec == n_sec - 1).astype(jnp.int32) if n_sec > 1 else jnp.int32(0)

    def opens(p):
        return ((p == 0) & (first_opens == 1)) | ((p == n_patch - 1) & (last_opens == 1))

    opener = opens(patch)
    openers_beside = first_opens * last_opens
    expected = (n_lev - 1) + jnp.where(opener, openers_beside, n_patch - 1)
    for side in range(2):
        s, p, lower, higher = beside(side)
        same = jnp.logical_not(lower | higher)

        @pl.when(higher | (same & (opener | jnp.logical_not(opens(p)))))
        def _(s=s, p=p):
            for step in (-1, 0, 1):
                greet((s, p, level_of(step)))

        expected = expected + jnp.where(lower | (same & jnp.logical_not(opener)), 3, 0)
    for i in range(1, n_lev):
        greet((sec, patch, level_of(i)))

    def greet_patch(i, carry):
        other = lax.rem(patch + i, n_patch)

        @pl.when(opener | jnp.logical_not(opens(other)))
        def _():
            greet((sec, other, lev))

        return carry

    lax.fori_loop(1, n_patch, greet_patch, 0)

    small = [
        (offs, offs_v), (edge, edge_v), (rates, rates_s), (owners, owners_v),
        (mixing, mix_v), (forcing_mix, fmix_v), (mask, mask_v), (ocean, ocean_v), (weights, weights_v),
    ]
    loads = [pltpu.make_async_copy(a, b, in_sem.at[i]) for i, (a, b) in enumerate(small)]
    for i in (0, 1):
        loads[i].start()
    atm_loads = [
        pltpu.make_async_copy(atm.at[t], ring.at[t, 0:klev, LANES : LANES + ncol], atm_sem.at[t])
        for t in range(ntr)
    ]
    for load in atm_loads:
        load.start()
    for load in loads[2:]:
        load.start()

    loads[0].wait()
    loads[1].wait()
    offsets, exchange = offs_v[...], edge_v[...]
    total = jnp.zeros((1, ncol), F32)
    for i, delta in enumerate(DELTAS):
        part = jnp.sum(jnp.where(offsets == delta, exchange, 0.0), axis=0, keepdims=True)
        total = total + part
        coef[i, :, LANES : LANES + ncol] = jnp.broadcast_to(part, (8, ncol))
    coef[4, :, LANES : LANES + ncol] = jnp.broadcast_to(1.0 - total, (8, ncol))

    lane = lax.broadcasted_iota(jnp.int32, (8, LANES), 1)
    row = lax.broadcasted_iota(jnp.int32, (8, LANES), 0)
    coef_lane = 2 * ntr * HALO
    for load in atm_loads:
        load.wait()
    first = jnp.zeros((8, LANES), F32)
    last = jnp.zeros((8, LANES), F32)
    for t in range(ntr):
        for k in range(2):
            at = (2 * t + k) * HALO
            here = (lane >= at) & (lane < at + HALO)
            a = ring[t, 8 * k : 8 * k + 8, LANES : 2 * LANES]
            b = ring[t, 8 * k : 8 * k + 8, ncol : ncol + LANES]
            first = jnp.where(here, pltpu.roll(a, at, 1) if at else a, first)
            last = jnp.where(here, pltpu.roll(b, at + HALO, 1), last)
    here = (lane >= coef_lane) & (lane < coef_lane + HALO)
    for i in range(4):
        a = coef[i, :, LANES : 2 * LANES]
        b = coef[i, :, ncol : ncol + LANES]
        first = jnp.where(here & (row == i), pltpu.roll(a, coef_lane, 1), first)
        last = jnp.where(here & (row == i), pltpu.roll(b, coef_lane + HALO, 1), last)
    edge_send[0] = first
    edge_send[1] = last

    pl.semaphore_wait(barrier, expected)

    def send_edge(side):
        s, p, _, _ = beside(side)
        for step in (0, -1, 1):
            pltpu.make_async_remote_copy(
                src_ref=edge_send.at[side],
                dst_ref=edge_recv.at[1 - side, 1 - step],
                send_sem=edge_sem.at[0],
                recv_sem=edge_sem.at[2 - side],
                device_id=(s, p, level_of(step)),
                device_id_type=MESH,
            ).start()

    def answer(where):
        pl.semaphore_signal(answer_sem, inc=1, device_id=where, device_id_type=MESH)

    for side in range(2):
        s, p, lower, higher = beside(side)
        same = jnp.logical_not(lower | higher)

        @pl.when(lower | (same & jnp.logical_not(opener)))
        def _(side=side):
            send_edge(side)

        @pl.when(same & jnp.logical_not(opener) & opens(p))
        def _(s=s, p=p):
            for step in (-1, 0, 1):
                answer((s, p, level_of(step)))

    for p in (0, n_patch - 1):
        @pl.when(jnp.logical_not(opener) & opens(jnp.int32(p)))
        def _(p=p):
            answer((sec, p, lev))

    def to_lower(t):
        return pltpu.make_async_remote_copy(
            src_ref=atm.at[t, 0:HALO, :],
            dst_ref=ring.at[t, klev : klev + HALO, LANES : LANES + ncol],
            send_sem=lev_send_sem.at[0, t],
            recv_sem=lev_up_sem.at[t],
            device_id=(sec, patch, level_of(-1)),
            device_id_type=MESH,
        )

    def to_upper(t):
        return pltpu.make_async_remote_copy(
            src_ref=atm.at[t, klev - HALO : klev, :],
            dst_ref=ring.at[t, klev + HALO : rows, LANES : LANES + ncol],
            send_sem=lev_send_sem.at[1, t],
            recv_sem=lev_down_sem.at[t],
            device_id=(sec, patch, level_of(1)),
            device_id_type=MESH,
        )

    @pl.when(lev > 0)
    def _():
        for t in range(ntr):
            to_lower(t).start()

    @pl.when(lev < n_lev - 1)
    def _():
        for t in range(ntr):
            to_upper(t).start()

    @pl.when(lev == 0)
    def _():
        ring[:, klev + HALO : rows, LANES : LANES + ncol] = jnp.zeros((ntr, HALO, ncol), F32)

    @pl.when(lev == n_lev - 1)
    def _():
        ring[:, klev : klev + HALO, LANES : LANES + ncol] = jnp.zeros((ntr, HALO, ncol), F32)

    for load in loads[2:]:
        load.wait()
    owned = owners_v[...]
    hot = (lax.broadcasted_iota(jnp.int32, (n_patch, block), 0) == owned).astype(F32)
    cols_hot[...] = hot
    earlier = (
        lax.broadcasted_iota(jnp.int32, (block, block), 0) < lax.broadcasted_iota(jnp.int32, (block, block), 1)
    ).astype(F32).astype(BF16)
    rank = jnp.dot(hot.astype(BF16), earlier, preferred_element_type=F32)
    slot = jnp.sum(rank * hot, axis=0, keepdims=True).astype(jnp.int32)
    lane_slot = lax.rem(lax.broadcasted_iota(jnp.int32, (LANES, block), 0), slots)
    slot_hot[...] = (lane_slot == slot).astype(F32).astype(BF16)
    for t in range(ntr):
        mix_cols[t] = jnp.broadcast_to(mix_v[:, t : t + 1], (mixing.shape[0], block))

    state = ocean_v[...]
    nol = state.shape[1]
    level = lax.broadcasted_iota(jnp.int32, state.shape, 1)
    above = jnp.where(level < nol - 1, pltpu.roll(state, nol - 1, 1) - state, 0.0)
    below = jnp.where(level > 0, pltpu.roll(state, 1, 1) - state, 0.0)
    base_v[...] = state + 0.2 * above + 0.2 * below

    @pl.when(opener)
    def _():
        pl.semaphore_wait(answer_sem, n_patch - 1 - openers_beside + 3)
        for side in range(2):
            _, _, lower, higher = beside(side)

            @pl.when(jnp.logical_not(lower | higher))
            def _(side=side):
                send_edge(side)

    ring_row = lax.broadcasted_iota(jnp.int32, (rows, LANES), 0)
    k = lev * klev + jnp.where(ring_row < klev + HALO, ring_row, ring_row - rows)
    inside = (k >= 0) & (k < alev)
    vertical = (
        3.0
        - (k < 1).astype(F32) - 0.5 * (k < 2).astype(F32)
        - (k > alev - 2).astype(F32) - 0.5 * (k > alev - 3).astype(F32)
    )
    inside_halo = inside[klev:, :]

    def halo_lane(side):
        return (1 - side) * (LANES - HALO)

    def halo_at(side):
        return pl.multiple_of(side * (LANES + ncol), LANES)

    def across(x, times):
        return jnp.concatenate([x] * times, axis=1) if times > 1 else x

    def down(x):
        return jnp.concatenate([x] * (rows // 8), axis=0)

    def stencil(x, at, first, tiles, rate, rate_vertical):
        width = tiles * LANES
        part = slice(first * LANES, first * LANES + width)
        middle = x[:, part]
        columns = pl.ds(at, width)
        out = middle * (down(coef[4, :, columns]) - across(rate_vertical, tiles))
        for i, delta in enumerate(DELTAS):
            moved = pltpu.roll(x, (-delta) % x.shape[1], 1)[:, part]
            out = out + down(coef[i, :, columns]) * moved
        one = pltpu.roll(middle, 1, 0) + pltpu.roll(middle, rows - 1, 0)
        two = pltpu.roll(middle, 2, 0) + pltpu.roll(middle, rows - 2, 0)
        return out + rate * (one + 0.5 * two)

    def masked(x, tiles):
        return jnp.concatenate(
            [x[:klev], jnp.where(across(inside_halo, tiles), x[klev:], 0.0)], axis=0
        )

    n_tiles = ncol // LANES
    per_block = block // LANES
    n_a = sums_a.shape[2]

    def step_1(t, first, tiles, rate, rate_vertical):
        at = LANES * (1 + first)
        x = ring[t, :, at - LANES : at + (tiles + 1) * LANES]
        step1[:, at : at + tiles * LANES] = masked(stencil(x, at, 1, tiles, rate, rate_vertical), tiles)

    def step_2(t, first, tiles, rate, rate_vertical, sums, at_row):
        at = LANES * (1 + first)
        x = step1[:, at - LANES : at + (tiles + 1) * LANES]
        out = stencil(x, at, 1, tiles, rate, rate_vertical)[:klev]
        result[t, :, at - LANES : at + (tiles - 1) * LANES] = out
        column_sums = jnp.sum(out, axis=0, keepdims=True)
        for i in range(tiles):
            d, half = divmod(first + i, per_block)
            sums[d, half, pl.ds(at_row, 1), :] = column_sums[:, i * LANES : (i + 1) * LANES]

    def inner(t, sums, at_row):
        @pl.when(lev < n_lev - 1)
        def _():
            to_lower(t).wait_recv()

        @pl.when(lev > 0)
        def _():
            to_upper(t).wait_recv()

        rate = rates_s[t]
        rate_vertical = rate * vertical
        for first in range(0, n_tiles, 4):
            step_1(t, first, 4, rate, rate_vertical)
        for first in range(0, n_tiles, 4):
            low, high = max(first, 1), min(first + 4, n_tiles - 1)
            step_2(t, low, high - low, rate, rate_vertical, sums, at_row)

    def outer(side, t, sums, at_row):
        rate = rates_s[t]
        rate_vertical = rate * vertical
        low, high = 2 * HALO * t, 2 * HALO * t + HALO

        def moved(level, lanes_at):
            return pltpu.roll(edge_recv[side, level], lax.rem(halo_lane(side) - lanes_at + LANES, LANES), 1)

        halo = jnp.concatenate(
            [
                moved(1, low),
                moved(1, high),
                jnp.where(inside_halo, jnp.where(row < HALO, moved(2, low), moved(0, high)), 0.0),
            ],
            axis=0,
        )
        ring[t, :, pl.ds(halo_at(side), LANES)] = halo
        start = pl.multiple_of(side * (wide - 3 * LANES), LANES)
        x = ring[t, :, pl.ds(start, 3 * LANES)]
        x = masked(stencil(x, start, 0, 3, rate, rate_vertical), 3)
        out = stencil(x, pl.multiple_of(start + LANES, LANES), 1, 1, rate, rate_vertical)[:klev]
        result[t, :, pl.ds(pl.multiple_of(side * (ncol - LANES), LANES), LANES)] = out
        sums[side * (n_lev - 1), side * (per_block - 1), pl.ds(at_row, 1), :] = jnp.sum(out, axis=0, keepdims=True)

    def send_sums(d):
        @pl.when(lev != d)
        def _():
            for which, (sums, got) in enumerate(((sums_a, got_a), (sums_b, got_b))):
                pltpu.make_async_remote_copy(
                    src_ref=sums.at[d],
                    dst_ref=got.at[lax.rem(lev - d + n_lev, n_lev) - 1],
                    send_sem=sum_sem.at[0, which],
                    recv_sem=sum_sem.at[1, which],
                    device_id=(sec, patch, d),
                    device_id_type=MESH,
                ).start()

    def all_tracers(step):
        def with_a(t, carry):
            step(t, sums_a, t)
            return carry

        def with_b(t, carry):
            step(t, sums_b, t - n_a)
            return carry

        lax.fori_loop(0, n_a, with_a, 0)
        lax.fori_loop(n_a, ntr, with_b, 0)

    all_tracers(inner)
    for d in range(1, n_lev - 1):
        send_sums(d)

    def one_side(i, carry):
        side = lax.rem(i + (patch == 0).astype(jnp.int32), 2)
        here = edge_recv.at[side]
        pltpu.make_async_copy(here, here, edge_sem.at[1 + side]).wait()

        @pl.when(beside(side)[3])
        def _():
            send_edge(side)

        around = pltpu.roll(edge_recv[side, 1], lax.rem(halo_lane(side) - coef_lane + LANES, LANES), 1)
        total = jnp.zeros((1, LANES), F32)
        columns = pl.ds(halo_at(side), LANES)
        for k in range(4):
            part = around[k : k + 1, :]
            total = total + part
            coef[k, :, columns] = jnp.broadcast_to(part, (8, LANES))
        coef[4, :, columns] = jnp.broadcast_to(1.0 - total, (8, LANES))
        all_tracers(functools.partial(outer, side))
        send_sums(side * (n_lev - 1))
        return carry

    lax.fori_loop(0, 2, one_side, 0)

    pick = (
        lax.broadcasted_iota(jnp.int32, (ntr, ntr), 0) == lax.broadcasted_iota(jnp.int32, (ntr, ntr), 1)
    )
    fmix = fmix_v[...]
    fmix_cols = [
        jnp.sum(jnp.where(pick, jnp.broadcast_to(fmix[v : v + 1, :], (ntr, ntr)), 0.0), axis=1, keepdims=True)
        for v in range(2)
    ]

    def level_sums(sums, got, which):
        pltpu.make_async_copy(got, got, sum_sem.at[1, which]).wait()
        out = sums[lev]
        for i in range(n_lev - 1):
            out = out + got[i]
        return jnp.concatenate([out[i] for i in range(per_block)], axis=1)

    mean_a = level_sums(sums_a, got_a, 0) * (1.0 / alev)
    mixed = jnp.zeros((mixing.shape[0], block), F32)
    for t in range(n_a):
        mixed = mixed + mix_cols[t] * mean_a[t : t + 1, :]
    mean_b = level_sums(sums_b, got_b, 1) * (1.0 / alev)
    for t in range(n_a, ntr):
        mixed = mixed + mix_cols[t] * mean_b[t - n_a : t - n_a + 1, :]
    flux = jnp.tanh(mixed)
    hot = cols_hot[...]
    parts = []
    for v in range(2):
        forced = jnp.sum(fmix_cols[v] * flux, axis=0, keepdims=True)
        parts += [(hot * piece.astype(F32)).astype(BF16) for piece in split_2(forced)]
    slot_map = slot_hot[...]
    out = lax.dot_general(
        jnp.concatenate(parts, axis=0), slot_map, (((1,), (1,)), ((), ())), preferred_element_type=F32
    )
    outgoing = [out[2 * v * n_patch : (2 * v + 1) * n_patch] + out[(2 * v + 1) * n_patch : (2 * v + 2) * n_patch] for v in range(2)]
    for v in range(2):
        flux_send[:, v * LANES : (v + 1) * LANES] = outgoing[v]

    across_patch = 4
    down_patch = n_patch // across_patch

    def far_first(i):
        def moved(i, n):
            half = lax.div(i + 1, 2)
            return n // 2 + jnp.where(lax.rem(i, 2) == 1, -half, half)

        y = lax.div(patch, across_patch) + moved(lax.div(i, across_patch), down_patch)
        x = lax.rem(patch, across_patch) + moved(lax.rem(i, across_patch), across_patch)
        return lax.rem(y, down_patch) * across_patch + lax.rem(x, across_patch)

    def send_flux(i, carry):
        other = far_first(i)
        pltpu.make_async_remote_copy(
            src_ref=flux_send.at[pl.ds(other, 1), :],
            dst_ref=flux_recv.at[pl.ds(patch, 1), :],
            send_sem=flux_sem.at[0],
            recv_sem=flux_sem.at[1],
            device_id=(sec, other, lev),
            device_id_type=MESH,
        ).start()
        return carry

    lax.fori_loop(0, n_patch - 1, send_flux, 0)
    own_row = pl.ds(patch, 1)
    pltpu.make_async_copy(flux_send.at[own_row, :], flux_recv.at[own_row, :], flux_sem.at[1]).start()
    ocean_cells = mask_v[...].astype(F32)
    pltpu.make_async_copy(flux_recv, flux_recv, flux_sem.at[1]).wait()

    groups = n_patch * slots // LANES
    received = []
    for v in range(2):
        pieces = []
        for g in range(groups):
            tile = flux_recv[g * copies : (g + 1) * copies, v * LANES : (v + 1) * LANES]
            pieces.append(jnp.sum(jnp.where(lax.div(lane, slots) == row, tile, 0.0), axis=0, keepdims=True))
        received.append(jnp.concatenate(pieces, axis=1))
    w = weights_v[...]

    def stacked(values):
        at = lax.broadcasted_iota(jnp.int32, (16, values[0].shape[1]), 0)
        out = jnp.zeros((16, values[0].shape[1]), F32)
        for i, value in enumerate(values):
            out = jnp.where(at == i, value.astype(F32), out)
        return out.astype(BF16)

    sums = jnp.dot(stacked([*split_2(received[0]), *split_2(received[1])]), w, preferred_element_type=F32)
    forcing = [(sums[2 * v : 2 * v + 1] + sums[2 * v + 1 : 2 * v + 2]) * ocean_cells for v in range(2)]
    warmth = (base_v[0, 0:1, :] + forcing[0]) * ocean_cells
    back = lax.dot_general(
        stacked([*split_2(warmth)]), w, (((1,), (1,)), ((), ())), preferred_element_type=F32
    )
    back = back[0:1] + back[1:2]
    for g in range(groups):
        back_send[g : g + 1, :] = back[:, g * LANES : (g + 1) * LANES]

    def send_back(i, carry):
        other = far_first(i)
        pltpu.make_async_remote_copy(
            src_ref=back_send.at[pl.ds(lax.div(other, copies), 1), :],
            dst_ref=back_recv.at[pl.ds(patch, 1), :],
            send_sem=back_sem.at[0],
            recv_sem=back_sem.at[1],
            device_id=(sec, other, lev),
            device_id_type=MESH,
        ).start()
        return carry

    lax.fori_loop(0, n_patch - 1, send_back, 0)
    pltpu.make_async_copy(
        back_send.at[pl.ds(lax.div(patch, copies), 1), :], back_recv.at[own_row, :], back_sem.at[1]
    ).start()

    depth = lax.broadcasted_iota(jnp.int32, (nol, block), 0).astype(F32)
    profile = jnp.exp(-depth / 8.0)
    for v in range(2):
        ocean_new[v] = base_v[v] + profile * forcing[v]

    pltpu.make_async_copy(back_recv, back_recv, back_sem.at[1]).wait()
    at_lane = lax.broadcasted_iota(jnp.int32, (n_patch, LANES), 1)
    own = lax.div(at_lane, slots) == lax.rem(patch, copies)
    returned = jnp.where(own, back_recv[...], 0.0)
    values = jnp.dot(jnp.concatenate(split_2(returned), axis=0), slot_map, preferred_element_type=F32)
    surface_new[...] = jnp.sum((values[:n_patch] + values[n_patch:]) * hot, axis=0, keepdims=True)

    pltpu.make_async_copy(edge_recv, edge_recv, edge_sem.at[0]).wait()

    @pl.when(lev > 0)
    def _():
        for t in range(ntr):
            to_lower(t).wait_send()

    @pl.when(lev < n_lev - 1)
    def _():
        for t in range(ntr):
            to_upper(t).wait_send()

    pltpu.make_async_copy(got_a, got_a, sum_sem.at[0, 0]).wait()
    pltpu.make_async_copy(got_b, got_b, sum_sem.at[0, 1]).wait()
    count = n_patch // 2
    while count:
        for ref, sem in ((flux_recv, flux_sem), (back_recv, back_sem)):
            some = ref.at[pl.ds(0, count), :]
            pltpu.make_async_copy(some, some, sem.at[0]).wait()
        count //= 2


def store(a, b, c, a_out, b_out, c_out, sem):
    copies = [pltpu.make_async_copy(x, y, sem.at[i]) for i, (x, y) in enumerate(((a, a_out), (b, b_out), (c, c_out)))]
    for copy in copies:
        copy.start()
    for copy in copies:
        copy.wait()


def solution(mesh):
    dims = tuple(mesh.shape[a] for a in ("sec", "patch", "lev"))
    n_sec, n_patch, n_lev = dims

    def per_device(atm, offs, edge, rates, mixing, owners, weights, mask, ocean, forcing_mix):
        ntr, klev, ncol = atm.shape
        rows, wide = klev + 2 * HALO, ncol + 2 * LANES
        block = ncol // n_lev
        nflux = mixing.shape[0]
        owners, mask = owners.reshape(1, -1), mask.reshape(1, -1)
        dma = pltpu.SemaphoreType.DMA
        vmem = pltpu.VMEM
        any_space = pl.BlockSpec(memory_space=pltpu.HBM)
        in_vmem = pl.BlockSpec(memory_space=pltpu.VMEM)
        operands = [
            pltpu.with_memory_space_constraint(x, pltpu.HBM)
            for x in (atm, offs, edge, rates, mixing, owners, weights, mask, ocean, forcing_mix)
        ]
        out = pl.pallas_call(
            functools.partial(interval, dims),
            out_shape=(
                jax.ShapeDtypeStruct(atm.shape, F32),
                jax.ShapeDtypeStruct(ocean.shape, F32),
                jax.ShapeDtypeStruct((1, block), F32),
            ),
            in_specs=[any_space] * 10,
            out_specs=(in_vmem,) * 3,
            scratch_shapes=[
                vmem((ntr, rows, wide), F32),
                vmem((rows, wide), F32),
                vmem((5, 8, wide), F32),
                vmem(offs.shape, jnp.int32),
                vmem(edge.shape, F32),
                pltpu.SMEM(rates.shape, F32),
                vmem(mixing.shape, F32),
                vmem(owners.shape, jnp.int32),
                vmem(weights.shape, BF16),
                vmem(mask.shape, jnp.int32),
                vmem(ocean.shape, F32),
                vmem(ocean.shape, F32),
                vmem(forcing_mix.shape, F32),
                vmem((2, 8, LANES), F32),
                vmem((2, 3, 8, LANES), F32),
                vmem((n_lev, block // LANES, 8, LANES), F32),
                vmem((n_lev, block // LANES, ntr - 8, LANES), F32),
                vmem((n_lev - 1, block // LANES, 8, LANES), F32),
                vmem((n_lev - 1, block // LANES, ntr - 8, LANES), F32),
                vmem((n_patch, 2 * LANES), F32),
                vmem((n_patch, 2 * LANES), F32),
                vmem((weights.shape[0] // LANES, LANES), F32),
                vmem((n_patch, LANES), F32),
                vmem((n_patch, block), F32),
                vmem((LANES, block), BF16),
                vmem((ntr, nflux, block), F32),
                dma((ntr,)),
                dma((9,)),
                dma((3,)),
                pltpu.SemaphoreType.REGULAR,
                dma((2, ntr)),
                dma((ntr,)),
                dma((ntr,)),
                dma((2, 2)),
                dma((2,)),
                dma((2,)),
            ],
            compiler_params=pltpu.CompilerParams(
                collective_id=0, has_side_effects=True, vmem_limit_bytes=40 * 1024 * 1024
            ),
            name="interval",
        )(*operands)
        out = pl.pallas_call(
            store,
            out_shape=tuple(jax.ShapeDtypeStruct(x.shape, F32) for x in out),
            in_specs=[in_vmem] * 3,
            out_specs=(any_space,) * 3,
            scratch_shapes=[dma((3,))],
            compiler_params=pltpu.CompilerParams(vmem_limit_bytes=8 * 1024 * 1024),
            name="store",
        )(*out)
        return out[0], out[1], out[2].reshape(-1)

    in_specs = (
        P(None, "lev", ("sec", "patch")),
        P(None, ("sec", "patch")),
        P(None, ("sec", "patch")),
        P(),
        P(),
        P(("sec", "patch", "lev"), None),
        P(None, ("sec", "patch", "lev")),
        P(("sec", "patch", "lev")),
        P(None, None, ("sec", "patch", "lev")),
        P(),
    )
    out_specs = (
        P(None, "lev", ("sec", "patch")),
        P(None, None, ("sec", "patch", "lev")),
        P(("sec", "patch", "lev")),
    )
    return jax.shard_map(per_device, mesh=mesh, in_specs=in_specs, out_specs=out_specs, check_vma=False)
```

```python
import functools
import jax
import jax.numpy as jnp
from jax import lax
from jax.experimental import pallas as pl
from jax.experimental.pallas import tpu as pltpu
from jax.sharding import PartitionSpec as P

F32 = jnp.float32
BF16 = jnp.bfloat16
MESH = pl.DeviceIdType.MESH
DELTAS = (-2, -1, 1, 2)
LANES = 128
HALO = 4
GROUP = 3 * HALO


def split_2(x):
    high = x.astype(BF16)
    return high, (x - high.astype(F32)).astype(BF16)


def interval(
    dims,
    atm, offs, edge, rates, mixing, owners, weights, mask, ocean, forcing_mix,
    result, ocean_new, surface_new,
    ring, step1, coef, offs_v, edge_v, rates_s, mix_v, owners_v, weights_v, mask_v, ocean_v, base_v, fmix_v,
    edge_send, edge_recv, own_edge, outer_v, sums_a, sums_b, got_a, got_b, flux_send, flux_recv, back_send, back_recv,
    cols_hot, slot_hot, mix_cols,
    atm_sem, in_sem, edge_sem, answer_sem, lev_send_sem, lev_up_sem, lev_down_sem, sum_sem, flux_sem, back_sem,
):
    n_sec, n_patch, n_lev = dims
    ntr, klev, ncol = atm.shape
    alev = klev * n_lev
    block = ncol // n_lev
    slots = weights.shape[0] // n_patch
    copies = LANES // slots
    wide = ncol + 2 * LANES
    rows = klev + 2 * HALO

    sec, patch, lev = lax.axis_index("sec"), lax.axis_index("patch"), lax.axis_index("lev")
    place = sec * n_patch + patch
    n_place = n_sec * n_patch

    def column_neighbour(step):
        other = lax.rem(place + step + n_place, n_place)
        return lax.div(other, n_patch), lax.rem(other, n_patch)

    def beside(side):
        s, p = column_neighbour(2 * side - 1)
        return s, p, s < sec, s > sec

    def level_of(step):
        return lax.rem(lev + step + n_lev, n_lev)

    barrier = pltpu.get_barrier_semaphore()

    def greet(where):
        pl.semaphore_signal(barrier, inc=1, device_id=where, device_id_type=MESH)

    first_opens = (sec > 0).astype(jnp.int32)
    last_opens = (sec == n_sec - 1).astype(jnp.int32) if n_sec > 1 else jnp.int32(0)

    def opens(p):
        return ((p == 0) & (first_opens == 1)) | ((p == n_patch - 1) & (last_opens == 1))

    opener = opens(patch)
    openers_beside = first_opens * last_opens
    expected = (n_lev - 1) + jnp.where(opener, openers_beside, n_patch - 1)
    for side in range(2):
        s, p, lower, higher = beside(side)
        same = jnp.logical_not(lower | higher)

        @pl.when(higher | (same & (opener | jnp.logical_not(opens(p)))))
        def _(s=s, p=p):
            for step in (-1, 0, 1):
                greet((s, p, level_of(step)))

        expected = expected + jnp.where(lower | (same & jnp.logical_not(opener)), 3, 0)
    for i in range(1, n_lev):
        greet((sec, patch, level_of(i)))

    def greet_patch(i, carry):
        other = lax.rem(patch + i, n_patch)

        @pl.when(opener | jnp.logical_not(opens(other)))
        def _():
            greet((sec, other, lev))

        return carry

    lax.fori_loop(1, n_patch, greet_patch, 0)

    small = [
        (offs, offs_v), (edge, edge_v), (rates, rates_s), (owners, owners_v),
        (mixing, mix_v), (forcing_mix, fmix_v), (mask, mask_v), (ocean, ocean_v), (weights, weights_v),
    ]
    loads = [pltpu.make_async_copy(a, b, in_sem.at[i]) for i, (a, b) in enumerate(small)]
    for i in (0, 1):
        loads[i].start()
    atm_loads = [
        pltpu.make_async_copy(atm.at[t], ring.at[t, 0:klev, LANES : LANES + ncol], atm_sem.at[t])
        for t in range(ntr)
    ]
    for load in atm_loads:
        load.start()
    for load in loads[2:]:
        load.start()

    loads[0].wait()
    loads[1].wait()
    offsets, exchange = offs_v[...], edge_v[...]
    total = jnp.zeros((1, ncol), F32)
    for i, delta in enumerate(DELTAS):
        part = jnp.sum(jnp.where(offsets == delta, exchange, 0.0), axis=0, keepdims=True)
        total = total + part
        coef[i, :, LANES : LANES + ncol] = jnp.broadcast_to(part, (8, ncol))
    coef[4, :, LANES : LANES + ncol] = jnp.broadcast_to(1.0 - total, (8, ncol))

    lane = lax.broadcasted_iota(jnp.int32, (8, LANES), 1)
    row = lax.broadcasted_iota(jnp.int32, (8, LANES), 0)
    for load in atm_loads:
        load.wait()

    def packed(of_tracer, source, width, target):
        out = jnp.zeros((8, LANES), F32)
        for t in range(ntr):
            at = GROUP * t + target
            shift = (at - source) % LANES
            x = of_tracer(t)
            out = jnp.where((lane >= at) & (lane < at + width), pltpu.roll(x, shift, 1) if shift else x, out)
        return out

    starts = (LANES, ncol)
    coef_rows = []
    for start in starts:
        out = jnp.zeros((8, LANES), F32)
        for i in range(4):
            out = jnp.where(row == i, coef[i, :, start : start + LANES], out)
        coef_rows.append(out)

    def at_border(side, k, source, width, target):
        if k == 3:
            return packed(lambda t: coef_rows[side], source, width, target)
        start = starts[side]
        return packed(lambda t: ring[t, 8 * k : 8 * k + 8, start : start + LANES], source, width, target)

    for i, k in enumerate((0, 1, 3)):
        edge_send[0, i] = at_border(0, k, 0, HALO, 2 * HALO)
        edge_send[1, i] = at_border(1, k, LANES - HALO, HALO, 0)
    own_edge[0, 3] = at_border(0, 3, 0, 2 * HALO, HALO)
    own_edge[1, 3] = at_border(1, 3, LANES - 2 * HALO, 2 * HALO, 0)

    pl.semaphore_wait(barrier, expected)

    def send_edge(side):
        s, p, _, _ = beside(side)
        for step in (0, -1, 1):
            pltpu.make_async_remote_copy(
                src_ref=edge_send.at[side],
                dst_ref=edge_recv.at[1 - side, 1 - step],
                send_sem=edge_sem.at[0],
                recv_sem=edge_sem.at[2 - side],
                device_id=(s, p, level_of(step)),
                device_id_type=MESH,
            ).start()

    def answer(where):
        pl.semaphore_signal(answer_sem, inc=1, device_id=where, device_id_type=MESH)

    for side in range(2):
        s, p, lower, higher = beside(side)
        same = jnp.logical_not(lower | higher)

        @pl.when(lower | (same & jnp.logical_not(opener)))
        def _(side=side):
            send_edge(side)

        @pl.when(same & jnp.logical_not(opener) & opens(p))
        def _(s=s, p=p):
            for step in (-1, 0, 1):
                answer((s, p, level_of(step)))

    for p in (0, n_patch - 1):
        @pl.when(jnp.logical_not(opener) & opens(jnp.int32(p)))
        def _(p=p):
            answer((sec, p, lev))

    def to_lower(t):
        return pltpu.make_async_remote_copy(
            src_ref=atm.at[t, 0:HALO, :],
            dst_ref=ring.at[t, klev : klev + HALO, LANES : LANES + ncol],
            send_sem=lev_send_sem.at[0, t],
            recv_sem=lev_up_sem.at[t],
            device_id=(sec, patch, level_of(-1)),
            device_id_type=MESH,
        )

    def to_upper(t):
        return pltpu.make_async_remote_copy(
            src_ref=atm.at[t, klev - HALO : klev, :],
            dst_ref=ring.at[t, klev + HALO : rows, LANES : LANES + ncol],
            send_sem=lev_send_sem.at[1, t],
            recv_sem=lev_down_sem.at[t],
            device_id=(sec, patch, level_of(1)),
            device_id_type=MESH,
        )

    @pl.when(lev > 0)
    def _():
        for t in range(ntr):
            to_lower(t).start()

    @pl.when(lev < n_lev - 1)
    def _():
        for t in range(ntr):
            to_upper(t).start()

    @pl.when(lev == 0)
    def _():
        ring[:, klev + HALO : rows, LANES : LANES + ncol] = jnp.zeros((ntr, HALO, ncol), F32)

    @pl.when(lev == n_lev - 1)
    def _():
        ring[:, klev : klev + HALO, LANES : LANES + ncol] = jnp.zeros((ntr, HALO, ncol), F32)

    for load in loads[2:]:
        load.wait()
    owned = owners_v[...]
    hot = (lax.broadcasted_iota(jnp.int32, (n_patch, block), 0) == owned).astype(F32)
    cols_hot[...] = hot
    earlier = (
        lax.broadcasted_iota(jnp.int32, (block, block), 0) < lax.broadcasted_iota(jnp.int32, (block, block), 1)
    ).astype(F32).astype(BF16)
    rank = jnp.dot(hot.astype(BF16), earlier, preferred_element_type=F32)
    slot = jnp.sum(rank * hot, axis=0, keepdims=True).astype(jnp.int32)
    lane_slot = lax.rem(lax.broadcasted_iota(jnp.int32, (LANES, block), 0), slots)
    slot_hot[...] = (lane_slot == slot).astype(F32).astype(BF16)
    for t in range(ntr):
        mix_cols[t] = jnp.broadcast_to(mix_v[:, t : t + 1], (mixing.shape[0], block))

    state = ocean_v[...]
    nol = state.shape[1]
    level = lax.broadcasted_iota(jnp.int32, state.shape, 1)
    above = jnp.where(level < nol - 1, pltpu.roll(state, nol - 1, 1) - state, 0.0)
    below = jnp.where(level > 0, pltpu.roll(state, 1, 1) - state, 0.0)
    base_v[...] = state + 0.2 * above + 0.2 * below

    @pl.when(opener)
    def _():
        pl.semaphore_wait(answer_sem, n_patch - 1 - openers_beside + 3)
        for side in range(2):
            _, _, lower, higher = beside(side)

            @pl.when(jnp.logical_not(lower | higher))
            def _(side=side):
                send_edge(side)

    ring_row = lax.broadcasted_iota(jnp.int32, (rows, LANES), 0)
    k = lev * klev + jnp.where(ring_row < klev + HALO, ring_row, ring_row - rows)
    inside = (k >= 0) & (k < alev)
    vertical = (
        3.0
        - (k < 1).astype(F32) - 0.5 * (k < 2).astype(F32)
        - (k > alev - 2).astype(F32) - 0.5 * (k > alev - 3).astype(F32)
    )
    inside_halo = inside[klev:, :]

    def across(x, times):
        return jnp.concatenate([x] * times, axis=1) if times > 1 else x

    def down(x):
        return jnp.concatenate([x] * (rows // 8), axis=0)

    def stencil(x, part, centre, sides, rate):
        middle = x[:, part]
        out = middle * centre
        for side, delta in zip(sides, DELTAS):
            out = out + side * pltpu.roll(x, (-delta) % x.shape[1], 1)[:, part]
        one = pltpu.roll(middle, 1, 0) + pltpu.roll(middle, rows - 1, 0)
        two = pltpu.roll(middle, 2, 0) + pltpu.roll(middle, rows - 2, 0)
        return out + rate * (one + 0.5 * two)

    def masked(x, tiles):
        return jnp.concatenate(
            [x[:klev], jnp.where(across(inside_halo, tiles), x[klev:], 0.0)], axis=0
        )

    per_block = block // LANES
    n_a = sums_a.shape[2]
    tiles = 8
    chunk = tiles * LANES

    def step(x, at, rate, rate_vertical):
        columns = slice(at, at + chunk)
        return stencil(
            x,
            slice(LANES, LANES + chunk),
            down(coef[4, :, columns]) - across(rate_vertical, tiles),
            [down(coef[i, :, columns]) for i in range(4)],
            rate,
        )

    def inner(t, sums, at_row):
        @pl.when(lev < n_lev - 1)
        def _():
            to_lower(t).wait_recv()

        @pl.when(lev > 0)
        def _():
            to_upper(t).wait_recv()

        rate = rates_s[t]
        rate_vertical = rate * vertical
        for at in range(LANES, LANES + ncol, chunk):
            x = ring[t, :, at - LANES : at + chunk + LANES]
            step1[:, at : at + chunk] = masked(step(x, at, rate, rate_vertical), tiles)
        for at in range(LANES, LANES + ncol, chunk):
            x = step1[:, at - LANES : at + chunk + LANES]
            out = step(x, at, rate, rate_vertical)[:klev]
            result[t, :, at - LANES : at - LANES + chunk] = out
            column_sums = jnp.sum(out, axis=0, keepdims=True)
            for i in range(tiles):
                d, half = divmod(at // LANES - 1 + i, per_block)
                sums[d, half, pl.ds(at_row, 1), :] = column_sums[:, i * LANES : (i + 1) * LANES]

    def send_sums(d):
        @pl.when(lev != d)
        def _():
            for which, (sums, got) in enumerate(((sums_a, got_a), (sums_b, got_b))):
                pltpu.make_async_remote_copy(
                    src_ref=sums.at[d],
                    dst_ref=got.at[lax.rem(lev - d + n_lev, n_lev) - 1],
                    send_sem=sum_sem.at[0, which],
                    recv_sem=sum_sem.at[1, which],
                    device_id=(sec, patch, d),
                    device_id_type=MESH,
                ).start()

    def all_tracers(step):
        def with_a(t, carry):
            step(t, sums_a, t)
            return carry

        def with_b(t, carry):
            step(t, sums_b, t - n_a)
            return carry

        lax.fori_loop(0, n_a, with_a, 0)
        lax.fori_loop(n_a, ntr, with_b, 0)

    all_tracers(inner)
    for d in range(1, n_lev - 1):
        send_sums(d)

    for k in range(3):
        own_edge[0, k] = at_border(0, k, 0, 2 * HALO, HALO)
        own_edge[1, k] = at_border(1, k, LANES - 2 * HALO, 2 * HALO, 0)
    in_group = lane
    lane_rate = jnp.zeros((8, LANES), F32)
    for t in range(ntr):
        here = lane >= GROUP * t
        in_group = jnp.where(here, lane - GROUP * t, in_group)
        lane_rate = jnp.where(here, rates_s[t], lane_rate)
    lane_rate = down(lane_rate)
    lane_vertical = lane_rate * vertical

    def one_side(i, carry):
        side = lax.rem(i + (patch == 0).astype(jnp.int32), 2)
        here = edge_recv.at[side]
        pltpu.make_async_copy(here, here, edge_sem.at[1 + side]).wait()

        @pl.when(beside(side)[3])
        def _():
            send_edge(side)

        theirs = (in_group < HALO * (1 - side)) | (in_group >= GROUP - HALO * side)
        corner = jnp.where(row < HALO, edge_recv[side, 2, 0], edge_recv[side, 0, 1])
        x = jnp.concatenate(
            [
                jnp.where(theirs, edge_recv[side, 1, 0], own_edge[side, 0]),
                jnp.where(theirs, edge_recv[side, 1, 1], own_edge[side, 1]),
                jnp.where(inside_halo, jnp.where(theirs, corner, own_edge[side, 2]), 0.0),
            ],
            axis=0,
        )
        factors = jnp.where(theirs, edge_recv[side, 1, 2], own_edge[side, 3])
        sides = [factors[k : k + 1, :] for k in range(4)]
        centre = 1.0 - (sides[0] + sides[1] + sides[2] + sides[3]) - lane_vertical
        for last in (False, True):
            x = stencil(x, slice(0, LANES), centre, sides, lane_rate)
            if not last:
                x = masked(x, 1)
        out = x[:klev]
        outer_v[side] = out
        column_sums = jnp.broadcast_to(jnp.sum(out, axis=0, keepdims=True), (8, LANES))
        first_lane = side * (LANES - HALO)
        changed = (lane >= first_lane) & (lane < first_lane + HALO)
        d, half = side * (n_lev - 1), side * (per_block - 1)
        for sums, t0, t1 in ((sums_a, 0, n_a), (sums_b, n_a, ntr)):
            values = jnp.zeros((8, LANES), F32)
            for t in range(t0, t1):
                values = jnp.where(row == t - t0, pltpu.roll(column_sums, (-GROUP * t - HALO) % LANES, 1), values)
            values = jnp.where(changed, pltpu.roll(values, first_lane, 1), 0.0)
            sums[d, half] = jnp.where(changed[: t1 - t0], values[: t1 - t0], sums[d, half])
        send_sums(d)
        return carry

    lax.fori_loop(0, 2, one_side, 0)
    lane_of_two = lax.broadcasted_iota(jnp.int32, (klev, LANES), 1)
    for side in range(2):
        out = outer_v[side]
        first_lane = side * (LANES - HALO)
        changed = (lane_of_two >= first_lane) & (lane_of_two < first_lane + HALO)
        columns = slice(side * (ncol - LANES), side * (ncol - LANES) + LANES)
        for t in range(ntr):
            shift = (first_lane - GROUP * t - HALO) % LANES
            result[t, :, columns] = jnp.where(changed, pltpu.roll(out, shift, 1), result[t, :, columns])

    pick = (
        lax.broadcasted_iota(jnp.int32, (ntr, ntr), 0) == lax.broadcasted_iota(jnp.int32, (ntr, ntr), 1)
    )
    fmix = fmix_v[...]
    fmix_cols = [
        jnp.sum(jnp.where(pick, jnp.broadcast_to(fmix[v : v + 1, :], (ntr, ntr)), 0.0), axis=1, keepdims=True)
        for v in range(2)
    ]

    def level_sums(sums, got, which):
        pltpu.make_async_copy(got, got, sum_sem.at[1, which]).wait()
        out = sums[lev]
        for i in range(n_lev - 1):
            out = out + got[i]
        return jnp.concatenate([out[i] for i in range(per_block)], axis=1)

    mean_a = level_sums(sums_a, got_a, 0) * (1.0 / alev)
    mixed = jnp.zeros((mixing.shape[0], block), F32)
    for t in range(n_a):
        mixed = mixed + mix_cols[t] * mean_a[t : t + 1, :]
    mean_b = level_sums(sums_b, got_b, 1) * (1.0 / alev)
    for t in range(n_a, ntr):
        mixed = mixed + mix_cols[t] * mean_b[t - n_a : t - n_a + 1, :]
    flux = jnp.tanh(mixed)
    hot = cols_hot[...]
    parts = []
    for v in range(2):
        forced = jnp.sum(fmix_cols[v] * flux, axis=0, keepdims=True)
        parts += [(hot * piece.astype(F32)).astype(BF16) for piece in split_2(forced)]
    slot_map = slot_hot[...]
    out = lax.dot_general(
        jnp.concatenate(parts, axis=0), slot_map, (((1,), (1,)), ((), ())), preferred_element_type=F32
    )
    outgoing = [out[2 * v * n_patch : (2 * v + 1) * n_patch] + out[(2 * v + 1) * n_patch : (2 * v + 2) * n_patch] for v in range(2)]
    for v in range(2):
        flux_send[:, v * LANES : (v + 1) * LANES] = outgoing[v]

    across_patch = 4
    down_patch = n_patch // across_patch

    def far_first(i):
        def moved(i, n):
            half = lax.div(i + 1, 2)
            return n // 2 + jnp.where(lax.rem(i, 2) == 1, -half, half)

        y = lax.div(patch, across_patch) + moved(lax.div(i, across_patch), down_patch)
        x = lax.rem(patch, across_patch) + moved(lax.rem(i, across_patch), across_patch)
        return lax.rem(y, down_patch) * across_patch + lax.rem(x, across_patch)

    def send_flux(i, carry):
        other = far_first(i)
        pltpu.make_async_remote_copy(
            src_ref=flux_send.at[pl.ds(other, 1), :],
            dst_ref=flux_recv.at[pl.ds(patch, 1), :],
            send_sem=flux_sem.at[0],
            recv_sem=flux_sem.at[1],
            device_id=(sec, other, lev),
            device_id_type=MESH,
        ).start()
        return carry

    lax.fori_loop(0, n_patch - 1, send_flux, 0)
    own_row = pl.ds(patch, 1)
    pltpu.make_async_copy(flux_send.at[own_row, :], flux_recv.at[own_row, :], flux_sem.at[1]).start()
    ocean_cells = mask_v[...].astype(F32)
    pltpu.make_async_copy(flux_recv, flux_recv, flux_sem.at[1]).wait()

    groups = n_patch * slots // LANES
    received = []
    for v in range(2):
        pieces = []
        for g in range(groups):
            tile = flux_recv[g * copies : (g + 1) * copies, v * LANES : (v + 1) * LANES]
            pieces.append(jnp.sum(jnp.where(lax.div(lane, slots) == row, tile, 0.0), axis=0, keepdims=True))
        received.append(jnp.concatenate(pieces, axis=1))
    w = weights_v[...]

    def stacked(values):
        at = lax.broadcasted_iota(jnp.int32, (16, values[0].shape[1]), 0)
        out = jnp.zeros((16, values[0].shape[1]), F32)
        for i, value in enumerate(values):
            out = jnp.where(at == i, value.astype(F32), out)
        return out.astype(BF16)

    sums = jnp.dot(stacked([*split_2(received[0]), *split_2(received[1])]), w, preferred_element_type=F32)
    forcing = [(sums[2 * v : 2 * v + 1] + sums[2 * v + 1 : 2 * v + 2]) * ocean_cells for v in range(2)]
    warmth = (base_v[0, 0:1, :] + forcing[0]) * ocean_cells
    back = lax.dot_general(
        stacked([*split_2(warmth)]), w, (((1,), (1,)), ((), ())), preferred_element_type=F32
    )
    back = back[0:1] + back[1:2]
    for g in range(groups):
        back_send[g : g + 1, :] = back[:, g * LANES : (g + 1) * LANES]

    def send_back(i, carry):
        other = far_first(i)
        pltpu.make_async_remote_copy(
            src_ref=back_send.at[pl.ds(lax.div(other, copies), 1), :],
            dst_ref=back_recv.at[pl.ds(patch, 1), :],
            send_sem=back_sem.at[0],
            recv_sem=back_sem.at[1],
            device_id=(sec, other, lev),
            device_id_type=MESH,
        ).start()
        return carry

    lax.fori_loop(0, n_patch - 1, send_back, 0)
    pltpu.make_async_copy(
        back_send.at[pl.ds(lax.div(patch, copies), 1), :], back_recv.at[own_row, :], back_sem.at[1]
    ).start()

    depth = lax.broadcasted_iota(jnp.int32, (nol, block), 0).astype(F32)
    profile = jnp.exp(-depth / 8.0)
    for v in range(2):
        ocean_new[v] = base_v[v] + profile * forcing[v]

    pltpu.make_async_copy(back_recv, back_recv, back_sem.at[1]).wait()
    at_lane = lax.broadcasted_iota(jnp.int32, (n_patch, LANES), 1)
    own = lax.div(at_lane, slots) == lax.rem(patch, copies)
    returned = jnp.where(own, back_recv[...], 0.0)
    values = jnp.dot(jnp.concatenate(split_2(returned), axis=0), slot_map, preferred_element_type=F32)
    surface_new[...] = jnp.sum((values[:n_patch] + values[n_patch:]) * hot, axis=0, keepdims=True)

    pltpu.make_async_copy(edge_recv, edge_recv, edge_sem.at[0]).wait()

    @pl.when(lev > 0)
    def _():
        for t in range(ntr):
            to_lower(t).wait_send()

    @pl.when(lev < n_lev - 1)
    def _():
        for t in range(ntr):
            to_upper(t).wait_send()

    pltpu.make_async_copy(got_a, got_a, sum_sem.at[0, 0]).wait()
    pltpu.make_async_copy(got_b, got_b, sum_sem.at[0, 1]).wait()
    count = n_patch // 2
    while count:
        for ref, sem in ((flux_recv, flux_sem), (back_recv, back_sem)):
            some = ref.at[pl.ds(0, count), :]
            pltpu.make_async_copy(some, some, sem.at[0]).wait()
        count //= 2


def store(a, b, c, a_out, b_out, c_out, sem):
    copies = [pltpu.make_async_copy(x, y, sem.at[i]) for i, (x, y) in enumerate(((a, a_out), (b, b_out), (c, c_out)))]
    for copy in copies:
        copy.start()
    for copy in copies:
        copy.wait()


def solution(mesh):
    dims = tuple(mesh.shape[a] for a in ("sec", "patch", "lev"))
    n_sec, n_patch, n_lev = dims

    def per_device(atm, offs, edge, rates, mixing, owners, weights, mask, ocean, forcing_mix):
        ntr, klev, ncol = atm.shape
        rows, wide = klev + 2 * HALO, ncol + 2 * LANES
        block = ncol // n_lev
        nflux = mixing.shape[0]
        owners, mask = owners.reshape(1, -1), mask.reshape(1, -1)
        dma = pltpu.SemaphoreType.DMA
        vmem = pltpu.VMEM
        any_space = pl.BlockSpec(memory_space=pltpu.HBM)
        in_vmem = pl.BlockSpec(memory_space=pltpu.VMEM)
        operands = [
            pltpu.with_memory_space_constraint(x, pltpu.HBM)
            for x in (atm, offs, edge, rates, mixing, owners, weights, mask, ocean, forcing_mix)
        ]
        out = pl.pallas_call(
            functools.partial(interval, dims),
            out_shape=(
                jax.ShapeDtypeStruct(atm.shape, F32),
                jax.ShapeDtypeStruct(ocean.shape, F32),
                jax.ShapeDtypeStruct((1, block), F32),
            ),
            in_specs=[any_space] * 10,
            out_specs=(in_vmem,) * 3,
            scratch_shapes=[
                vmem((ntr, rows, wide), F32),
                vmem((rows, wide), F32),
                vmem((5, 8, wide), F32),
                vmem(offs.shape, jnp.int32),
                vmem(edge.shape, F32),
                pltpu.SMEM(rates.shape, F32),
                vmem(mixing.shape, F32),
                vmem(owners.shape, jnp.int32),
                vmem(weights.shape, BF16),
                vmem(mask.shape, jnp.int32),
                vmem(ocean.shape, F32),
                vmem(ocean.shape, F32),
                vmem(forcing_mix.shape, F32),
                vmem((2, 3, 8, LANES), F32),
                vmem((2, 3, 3, 8, LANES), F32),
                vmem((2, 4, 8, LANES), F32),
                vmem((2, klev, LANES), F32),
                vmem((n_lev, block // LANES, 8, LANES), F32),
                vmem((n_lev, block // LANES, ntr - 8, LANES), F32),
                vmem((n_lev - 1, block // LANES, 8, LANES), F32),
                vmem((n_lev - 1, block // LANES, ntr - 8, LANES), F32),
                vmem((n_patch, 2 * LANES), F32),
                vmem((n_patch, 2 * LANES), F32),
                vmem((weights.shape[0] // LANES, LANES), F32),
                vmem((n_patch, LANES), F32),
                vmem((n_patch, block), F32),
                vmem((LANES, block), BF16),
                vmem((ntr, nflux, block), F32),
                dma((ntr,)),
                dma((9,)),
                dma((3,)),
                pltpu.SemaphoreType.REGULAR,
                dma((2, ntr)),
                dma((ntr,)),
                dma((ntr,)),
                dma((2, 2)),
                dma((2,)),
                dma((2,)),
            ],
            compiler_params=pltpu.CompilerParams(
                collective_id=0, has_side_effects=True, vmem_limit_bytes=40 * 1024 * 1024
            ),
            name="interval",
        )(*operands)
        out = pl.pallas_call(
            store,
            out_shape=tuple(jax.ShapeDtypeStruct(x.shape, F32) for x in out),
            in_specs=[in_vmem] * 3,
            out_specs=(any_space,) * 3,
            scratch_shapes=[dma((3,))],
            compiler_params=pltpu.CompilerParams(vmem_limit_bytes=8 * 1024 * 1024),
            name="store",
        )(*out)
        return out[0], out[1], out[2].reshape(-1)

    in_specs = (
        P(None, "lev", ("sec", "patch")),
        P(None, ("sec", "patch")),
        P(None, ("sec", "patch")),
        P(),
        P(),
        P(("sec", "patch", "lev"), None),
        P(None, ("sec", "patch", "lev")),
        P(("sec", "patch", "lev")),
        P(None, None, ("sec", "patch", "lev")),
        P(),
    )
    out_specs = (
        P(None, "lev", ("sec", "patch")),
        P(None, None, ("sec", "patch", "lev")),
        P(("sec", "patch", "lev")),
    )
    return jax.shard_map(per_device, mesh=mesh, in_specs=in_specs, out_specs=out_specs, check_vma=False)
```

```python
import functools
import jax
import jax.numpy as jnp
from jax import lax
from jax.experimental import pallas as pl
from jax.experimental.pallas import tpu as pltpu
from jax.sharding import PartitionSpec as P

F32 = jnp.float32
BF16 = jnp.bfloat16
MESH = pl.DeviceIdType.MESH
DELTAS = (-2, -1, 1, 2)
LANES = 128
HALO = 4
GROUP = 3 * HALO


def split_2(x):
    high = x.astype(BF16)
    return high, (x - high.astype(F32)).astype(BF16)


def interval(
    dims,
    atm, offs, edge, rates, mixing, owners, weights, mask, ocean, forcing_mix,
    result, ocean_new, surface_new,
    ring, step1, coef, offs_v, edge_v, rates_s, mix_v, owners_v, weights_v, mask_v, ocean_v, base_v, fmix_v,
    edge_send, edge_recv, own_edge, outer_v, sums_a, sums_b, got_a, got_b, flux_send, flux_recv, back_send, back_recv,
    cols_hot, slot_hot, mix_cols,
    atm_sem, in_sem, edge_sem, answer_sem, lev_send_sem, lev_up_sem, lev_down_sem, sum_sem, flux_sem, back_sem,
):
    n_sec, n_patch, n_lev = dims
    ntr, klev, ncol = atm.shape
    alev = klev * n_lev
    block = ncol // n_lev
    slots = weights.shape[0] // n_patch
    copies = LANES // slots
    wide = ncol + 2 * LANES
    rows = klev + 2 * HALO

    sec, patch, lev = lax.axis_index("sec"), lax.axis_index("patch"), lax.axis_index("lev")
    place = sec * n_patch + patch
    n_place = n_sec * n_patch

    def column_neighbour(step):
        other = lax.rem(place + step + n_place, n_place)
        return lax.div(other, n_patch), lax.rem(other, n_patch)

    def beside(side):
        s, p = column_neighbour(2 * side - 1)
        return s, p, s < sec, s > sec

    def level_of(step):
        return lax.rem(lev + step + n_lev, n_lev)

    small = [
        (offs, offs_v), (edge, edge_v), (rates, rates_s), (owners, owners_v),
        (mixing, mix_v), (forcing_mix, fmix_v), (mask, mask_v), (ocean, ocean_v), (weights, weights_v),
    ]
    loads = [pltpu.make_async_copy(a, b, in_sem.at[i]) for i, (a, b) in enumerate(small)]
    for i in (0, 1):
        loads[i].start()
    atm_loads = [
        pltpu.make_async_copy(atm.at[t], ring.at[t, 0:klev, LANES : LANES + ncol], atm_sem.at[t])
        for t in range(ntr)
    ]
    for load in atm_loads:
        load.start()

    barrier = pltpu.get_barrier_semaphore()

    def greet(where):
        pl.semaphore_signal(barrier, inc=1, device_id=where, device_id_type=MESH)

    first_opens = (sec > 0).astype(jnp.int32)
    last_opens = (sec == n_sec - 1).astype(jnp.int32) if n_sec > 1 else jnp.int32(0)

    def opens(p):
        return ((p == 0) & (first_opens == 1)) | ((p == n_patch - 1) & (last_opens == 1))

    opener = opens(patch)
    openers_beside = first_opens * last_opens
    expected = (n_lev - 1) + jnp.where(opener, openers_beside, n_patch - 1)
    for side in range(2):
        s, p, lower, higher = beside(side)
        same = jnp.logical_not(lower | higher)

        @pl.when(higher | (same & (opener | jnp.logical_not(opens(p)))))
        def _(s=s, p=p):
            for step in (-1, 0, 1):
                greet((s, p, level_of(step)))

        expected = expected + jnp.where(lower | (same & jnp.logical_not(opener)), 3, 0)
    for i in range(1, n_lev):
        greet((sec, patch, level_of(i)))

    def greet_patch(i, carry):
        other = lax.rem(patch + i, n_patch)

        @pl.when(opener | jnp.logical_not(opens(other)))
        def _():
            greet((sec, other, lev))

        return carry

    lax.fori_loop(1, n_patch, greet_patch, 0)

    for load in loads[2:]:
        load.start()

    loads[0].wait()
    loads[1].wait()
    offsets, exchange = offs_v[...], edge_v[...]
    total = jnp.zeros((1, ncol), F32)
    for i, delta in enumerate(DELTAS):
        part = jnp.sum(jnp.where(offsets == delta, exchange, 0.0), axis=0, keepdims=True)
        total = total + part
        coef[i, :, LANES : LANES + ncol] = jnp.broadcast_to(part, (8, ncol))
    coef[4, :, LANES : LANES + ncol] = jnp.broadcast_to(1.0 - total, (8, ncol))

    lane = lax.broadcasted_iota(jnp.int32, (8, LANES), 1)
    row = lax.broadcasted_iota(jnp.int32, (8, LANES), 0)
    for load in atm_loads:
        load.wait()

    def packed(of_tracer, source, width, target):
        out = jnp.zeros((8, LANES), F32)
        for t in range(ntr):
            at = GROUP * t + target
            shift = (at - source) % LANES
            x = of_tracer(t)
            out = jnp.where((lane >= at) & (lane < at + width), pltpu.roll(x, shift, 1) if shift else x, out)
        return out

    starts = (LANES, ncol)
    coef_rows = []
    for start in starts:
        out = jnp.zeros((8, LANES), F32)
        for i in range(4):
            out = jnp.where(row == i, coef[i, :, start : start + LANES], out)
        coef_rows.append(out)

    def at_border(side, k, source, width, target):
        if k == 3:
            return packed(lambda t: coef_rows[side], source, width, target)
        start = starts[side]
        return packed(lambda t: ring[t, 8 * k : 8 * k + 8, start : start + LANES], source, width, target)

    for i, k in enumerate((0, 1, 3)):
        edge_send[0, i] = at_border(0, k, 0, HALO, 2 * HALO)
        edge_send[1, i] = at_border(1, k, LANES - HALO, HALO, 0)
    own_edge[0, 3] = at_border(0, 3, 0, 2 * HALO, HALO)
    own_edge[1, 3] = at_border(1, 3, LANES - 2 * HALO, 2 * HALO, 0)

    pl.semaphore_wait(barrier, expected)

    def send_edge(side):
        s, p, _, _ = beside(side)
        away, there = edge_send.at[side], edge_recv.at[1 - side]
        for step, src, dst in (
            (0, away, there.at[0:3]),
            (1, away.at[1], there.at[3]),
            (-1, away.at[0], there.at[4]),
        ):
            pltpu.make_async_remote_copy(
                src_ref=src,
                dst_ref=dst,
                send_sem=edge_sem.at[0],
                recv_sem=edge_sem.at[2 - side],
                device_id=(s, p, level_of(step)),
                device_id_type=MESH,
            ).start()

    def answer(where):
        pl.semaphore_signal(answer_sem, inc=1, device_id=where, device_id_type=MESH)

    for side in range(2):
        s, p, lower, higher = beside(side)
        same = jnp.logical_not(lower | higher)

        @pl.when(lower | (same & jnp.logical_not(opener)))
        def _(side=side):
            send_edge(side)

        @pl.when(same & jnp.logical_not(opener) & opens(p))
        def _(s=s, p=p):
            for step in (-1, 0, 1):
                answer((s, p, level_of(step)))

    for p in (0, n_patch - 1):
        @pl.when(jnp.logical_not(opener) & opens(jnp.int32(p)))
        def _(p=p):
            answer((sec, p, lev))

    def to_lower(t):
        return pltpu.make_async_remote_copy(
            src_ref=atm.at[t, 0:HALO, :],
            dst_ref=ring.at[t, klev : klev + HALO, LANES : LANES + ncol],
            send_sem=lev_send_sem.at[0, t],
            recv_sem=lev_up_sem.at[t],
            device_id=(sec, patch, level_of(-1)),
            device_id_type=MESH,
        )

    def to_upper(t):
        return pltpu.make_async_remote_copy(
            src_ref=atm.at[t, klev - HALO : klev, :],
            dst_ref=ring.at[t, klev + HALO : rows, LANES : LANES + ncol],
            send_sem=lev_send_sem.at[1, t],
            recv_sem=lev_down_sem.at[t],
            device_id=(sec, patch, level_of(1)),
            device_id_type=MESH,
        )

    @pl.when(lev > 0)
    def _():
        for t in range(ntr):
            to_lower(t).start()

    @pl.when(lev < n_lev - 1)
    def _():
        for t in range(ntr):
            to_upper(t).start()

    @pl.when(lev == 0)
    def _():
        ring[:, klev + HALO : rows, LANES : LANES + ncol] = jnp.zeros((ntr, HALO, ncol), F32)

    @pl.when(lev == n_lev - 1)
    def _():
        ring[:, klev : klev + HALO, LANES : LANES + ncol] = jnp.zeros((ntr, HALO, ncol), F32)

    for load in loads[2:]:
        load.wait()
    owned = owners_v[...]
    hot = (lax.broadcasted_iota(jnp.int32, (n_patch, block), 0) == owned).astype(F32)
    cols_hot[...] = hot
    earlier = (
        lax.broadcasted_iota(jnp.int32, (block, block), 0) < lax.broadcasted_iota(jnp.int32, (block, block), 1)
    ).astype(F32).astype(BF16)
    rank = jnp.dot(hot.astype(BF16), earlier, preferred_element_type=F32)
    slot = jnp.sum(rank * hot, axis=0, keepdims=True).astype(jnp.int32)
    lane_slot = lax.rem(lax.broadcasted_iota(jnp.int32, (LANES, block), 0), slots)
    slot_hot[...] = (lane_slot == slot).astype(F32).astype(BF16)
    for t in range(ntr):
        mix_cols[t] = jnp.broadcast_to(mix_v[:, t : t + 1], (mixing.shape[0], block))

    state = ocean_v[...]
    nol = state.shape[1]
    level = lax.broadcasted_iota(jnp.int32, state.shape, 1)
    above = jnp.where(level < nol - 1, pltpu.roll(state, nol - 1, 1) - state, 0.0)
    below = jnp.where(level > 0, pltpu.roll(state, 1, 1) - state, 0.0)
    base_v[...] = state + 0.2 * above + 0.2 * below

    @pl.when(opener)
    def _():
        pl.semaphore_wait(answer_sem, n_patch - 1 - openers_beside + 3)
        for side in range(2):
            _, _, lower, higher = beside(side)

            @pl.when(jnp.logical_not(lower | higher))
            def _(side=side):
                send_edge(side)

    ring_row = lax.broadcasted_iota(jnp.int32, (rows, LANES), 0)
    k = lev * klev + jnp.where(ring_row < klev + HALO, ring_row, ring_row - rows)
    inside = (k >= 0) & (k < alev)
    vertical = (
        3.0
        - (k < 1).astype(F32) - 0.5 * (k < 2).astype(F32)
        - (k > alev - 2).astype(F32) - 0.5 * (k > alev - 3).astype(F32)
    )
    inside_halo = inside[klev:, :]

    def across(x, times):
        return jnp.concatenate([x] * times, axis=1) if times > 1 else x

    def down(x):
        return jnp.concatenate([x] * (rows // 8), axis=0)

    def stencil(x, part, centre, sides, rate):
        middle = x[:, part]
        out = middle * centre
        for side, delta in zip(sides, DELTAS):
            out = out + side * pltpu.roll(x, (-delta) % x.shape[1], 1)[:, part]
        one = pltpu.roll(middle, 1, 0) + pltpu.roll(middle, rows - 1, 0)
        two = pltpu.roll(middle, 2, 0) + pltpu.roll(middle, rows - 2, 0)
        return out + rate * (one + 0.5 * two)

    def masked(x, tiles):
        return jnp.concatenate(
            [x[:klev], jnp.where(across(inside_halo, tiles), x[klev:], 0.0)], axis=0
        )

    per_block = block // LANES
    n_a = sums_a.shape[2]
    tiles = 8
    chunk = tiles * LANES

    def step(x, at, rate, rate_vertical):
        columns = slice(at, at + chunk)
        return stencil(
            x,
            slice(LANES, LANES + chunk),
            down(coef[4, :, columns]) - across(rate_vertical, tiles),
            [down(coef[i, :, columns]) for i in range(4)],
            rate,
        )

    def inner(t, sums, at_row):
        @pl.when(lev < n_lev - 1)
        def _():
            to_lower(t).wait_recv()

        @pl.when(lev > 0)
        def _():
            to_upper(t).wait_recv()

        rate = rates_s[t]
        rate_vertical = rate * vertical
        for at in range(LANES, LANES + ncol, chunk):
            x = ring[t, :, at - LANES : at + chunk + LANES]
            step1[:, at : at + chunk] = masked(step(x, at, rate, rate_vertical), tiles)
        for at in range(LANES, LANES + ncol, chunk):
            x = step1[:, at - LANES : at + chunk + LANES]
            out = step(x, at, rate, rate_vertical)[:klev]
            result[t, :, at - LANES : at - LANES + chunk] = out
            column_sums = jnp.sum(out, axis=0, keepdims=True)
            for i in range(tiles):
                d, half = divmod(at // LANES - 1 + i, per_block)
                sums[d, half, pl.ds(at_row, 1), :] = column_sums[:, i * LANES : (i + 1) * LANES]

    def send_sums(d):
        @pl.when(lev != d)
        def _():
            for which, (sums, got) in enumerate(((sums_a, got_a), (sums_b, got_b))):
                pltpu.make_async_remote_copy(
                    src_ref=sums.at[d],
                    dst_ref=got.at[lax.rem(lev - d + n_lev, n_lev) - 1],
                    send_sem=sum_sem.at[0, which],
                    recv_sem=sum_sem.at[1, which],
                    device_id=(sec, patch, d),
                    device_id_type=MESH,
                ).start()

    def all_tracers(step):
        def with_a(t, carry):
            step(t, sums_a, t)
            return carry

        def with_b(t, carry):
            step(t, sums_b, t - n_a)
            return carry

        lax.fori_loop(0, n_a, with_a, 0)
        lax.fori_loop(n_a, ntr, with_b, 0)

    all_tracers(inner)
    for d in range(1, n_lev - 1):
        send_sums(d)

    for k in range(3):
        own_edge[0, k] = at_border(0, k, 0, 2 * HALO, HALO)
        own_edge[1, k] = at_border(1, k, LANES - 2 * HALO, 2 * HALO, 0)
    in_group = lane
    lane_rate = jnp.zeros((8, LANES), F32)
    for t in range(ntr):
        here = lane >= GROUP * t
        in_group = jnp.where(here, lane - GROUP * t, in_group)
        lane_rate = jnp.where(here, rates_s[t], lane_rate)
    lane_rate = down(lane_rate)
    lane_vertical = lane_rate * vertical

    def one_side(i, carry):
        side = lax.rem(i + (patch == 0).astype(jnp.int32), 2)
        here = edge_recv.at[side]
        pltpu.make_async_copy(here, here, edge_sem.at[1 + side]).wait()

        theirs = (in_group < HALO * (1 - side)) | (in_group >= GROUP - HALO * side)
        corner = jnp.where(row < HALO, edge_recv[side, 4], edge_recv[side, 3])
        x = jnp.concatenate(
            [
                jnp.where(theirs, edge_recv[side, 0], own_edge[side, 0]),
                jnp.where(theirs, edge_recv[side, 1], own_edge[side, 1]),
                jnp.where(inside_halo, jnp.where(theirs, corner, own_edge[side, 2]), 0.0),
            ],
            axis=0,
        )
        factors = jnp.where(theirs, edge_recv[side, 2], own_edge[side, 3])
        sides = [factors[k : k + 1, :] for k in range(4)]
        centre = 1.0 - (sides[0] + sides[1] + sides[2] + sides[3]) - lane_vertical
        for last in (False, True):
            x = stencil(x, slice(0, LANES), centre, sides, lane_rate)
            if not last:
                x = masked(x, 1)
        out = x[:klev]
        outer_v[side] = out
        column_sums = jnp.broadcast_to(jnp.sum(out, axis=0, keepdims=True), (8, LANES))
        first_lane = side * (LANES - HALO)
        changed = (lane >= first_lane) & (lane < first_lane + HALO)
        d, half = side * (n_lev - 1), side * (per_block - 1)
        for sums, t0, t1 in ((sums_a, 0, n_a), (sums_b, n_a, ntr)):
            values = jnp.zeros((8, LANES), F32)
            for t in range(t0, t1):
                values = jnp.where(row == t - t0, pltpu.roll(column_sums, (-GROUP * t - HALO) % LANES, 1), values)
            values = jnp.where(changed, pltpu.roll(values, first_lane, 1), 0.0)
            sums[d, half] = jnp.where(changed[: t1 - t0], values[: t1 - t0], sums[d, half])
        send_sums(d)

        @pl.when(beside(side)[3])
        def _():
            send_edge(side)

        return carry

    lax.fori_loop(0, 2, one_side, 0)
    lane_of_two = lax.broadcasted_iota(jnp.int32, (klev, LANES), 1)
    for side in range(2):
        out = outer_v[side]
        first_lane = side * (LANES - HALO)
        changed = (lane_of_two >= first_lane) & (lane_of_two < first_lane + HALO)
        columns = slice(side * (ncol - LANES), side * (ncol - LANES) + LANES)
        for t in range(ntr):
            shift = (first_lane - GROUP * t - HALO) % LANES
            result[t, :, columns] = jnp.where(changed, pltpu.roll(out, shift, 1), result[t, :, columns])

    pick = (
        lax.broadcasted_iota(jnp.int32, (ntr, ntr), 0) == lax.broadcasted_iota(jnp.int32, (ntr, ntr), 1)
    )
    fmix = fmix_v[...]
    fmix_cols = [
        jnp.sum(jnp.where(pick, jnp.broadcast_to(fmix[v : v + 1, :], (ntr, ntr)), 0.0), axis=1, keepdims=True)
        for v in range(2)
    ]

    def level_sums(sums, got, which):
        pltpu.make_async_copy(got, got, sum_sem.at[1, which]).wait()
        out = sums[lev]
        for i in range(n_lev - 1):
            out = out + got[i]
        return jnp.concatenate([out[i] for i in range(per_block)], axis=1)

    mean_a = level_sums(sums_a, got_a, 0) * (1.0 / alev)
    mixed = jnp.zeros((mixing.shape[0], block), F32)
    for t in range(n_a):
        mixed = mixed + mix_cols[t] * mean_a[t : t + 1, :]
    mean_b = level_sums(sums_b, got_b, 1) * (1.0 / alev)
    for t in range(n_a, ntr):
        mixed = mixed + mix_cols[t] * mean_b[t - n_a : t - n_a + 1, :]
    flux = jnp.tanh(mixed)
    hot = cols_hot[...]
    parts = []
    for v in range(2):
        forced = jnp.sum(fmix_cols[v] * flux, axis=0, keepdims=True)
        parts += [(hot * piece.astype(F32)).astype(BF16) for piece in split_2(forced)]
    slot_map = slot_hot[...]
    out = lax.dot_general(
        jnp.concatenate(parts, axis=0), slot_map, (((1,), (1,)), ((), ())), preferred_element_type=F32
    )
    outgoing = [out[2 * v * n_patch : (2 * v + 1) * n_patch] + out[(2 * v + 1) * n_patch : (2 * v + 2) * n_patch] for v in range(2)]
    for v in range(2):
        flux_send[:, v * LANES : (v + 1) * LANES] = outgoing[v]

    across_patch = 4
    down_patch = n_patch // across_patch

    def far_first(i):
        def moved(i, n):
            half = lax.div(i + 1, 2)
            return n // 2 + jnp.where(lax.rem(i, 2) == 1, -half, half)

        y = lax.div(patch, across_patch) + moved(lax.div(i, across_patch), down_patch)
        x = lax.rem(patch, across_patch) + moved(lax.rem(i, across_patch), across_patch)
        return lax.rem(y, down_patch) * across_patch + lax.rem(x, across_patch)

    def send_flux(i, carry):
        other = far_first(i)
        pltpu.make_async_remote_copy(
            src_ref=flux_send.at[pl.ds(other, 1), :],
            dst_ref=flux_recv.at[pl.ds(patch, 1), :],
            send_sem=flux_sem.at[0],
            recv_sem=flux_sem.at[1],
            device_id=(sec, other, lev),
            device_id_type=MESH,
        ).start()
        return carry

    lax.fori_loop(0, n_patch - 1, send_flux, 0)
    own_row = pl.ds(patch, 1)
    pltpu.make_async_copy(flux_send.at[own_row, :], flux_recv.at[own_row, :], flux_sem.at[1]).start()
    ocean_cells = mask_v[...].astype(F32)
    pltpu.make_async_copy(flux_recv, flux_recv, flux_sem.at[1]).wait()

    groups = n_patch * slots // LANES
    received = []
    for v in range(2):
        pieces = []
        for g in range(groups):
            tile = flux_recv[g * copies : (g + 1) * copies, v * LANES : (v + 1) * LANES]
            pieces.append(jnp.sum(jnp.where(lax.div(lane, slots) == row, tile, 0.0), axis=0, keepdims=True))
        received.append(jnp.concatenate(pieces, axis=1))
    w = weights_v[...]

    def stacked(values):
        at = lax.broadcasted_iota(jnp.int32, (16, values[0].shape[1]), 0)
        out = jnp.zeros((16, values[0].shape[1]), F32)
        for i, value in enumerate(values):
            out = jnp.where(at == i, value.astype(F32), out)
        return out.astype(BF16)

    sums = jnp.dot(stacked([*split_2(received[0]), *split_2(received[1])]), w, preferred_element_type=F32)
    forcing = [(sums[2 * v : 2 * v + 1] + sums[2 * v + 1 : 2 * v + 2]) * ocean_cells for v in range(2)]
    warmth = (base_v[0, 0:1, :] + forcing[0]) * ocean_cells
    back = lax.dot_general(
        stacked([*split_2(warmth)]), w, (((1,), (1,)), ((), ())), preferred_element_type=F32
    )
    back = back[0:1] + back[1:2]
    for g in range(groups):
        back_send[g : g + 1, :] = back[:, g * LANES : (g + 1) * LANES]

    def send_back(i, carry):
        other = far_first(i)
        pltpu.make_async_remote_copy(
            src_ref=back_send.at[pl.ds(lax.div(other, copies), 1), :],
            dst_ref=back_recv.at[pl.ds(patch, 1), :],
            send_sem=back_sem.at[0],
            recv_sem=back_sem.at[1],
            device_id=(sec, other, lev),
            device_id_type=MESH,
        ).start()
        return carry

    lax.fori_loop(0, n_patch - 1, send_back, 0)
    pltpu.make_async_copy(
        back_send.at[pl.ds(lax.div(patch, copies), 1), :], back_recv.at[own_row, :], back_sem.at[1]
    ).start()

    depth = lax.broadcasted_iota(jnp.int32, (nol, block), 0).astype(F32)
    profile = jnp.exp(-depth / 8.0)
    for v in range(2):
        ocean_new[v] = base_v[v] + profile * forcing[v]

    pltpu.make_async_copy(back_recv, back_recv, back_sem.at[1]).wait()
    at_lane = lax.broadcasted_iota(jnp.int32, (n_patch, LANES), 1)
    own = lax.div(at_lane, slots) == lax.rem(patch, copies)
    returned = jnp.where(own, back_recv[...], 0.0)
    values = jnp.dot(jnp.concatenate(split_2(returned), axis=0), slot_map, preferred_element_type=F32)
    surface_new[...] = jnp.sum((values[:n_patch] + values[n_patch:]) * hot, axis=0, keepdims=True)

    pltpu.make_async_copy(edge_recv, edge_recv, edge_sem.at[0]).wait()

    @pl.when(lev > 0)
    def _():
        for t in range(ntr):
            to_lower(t).wait_send()

    @pl.when(lev < n_lev - 1)
    def _():
        for t in range(ntr):
            to_upper(t).wait_send()

    pltpu.make_async_copy(got_a, got_a, sum_sem.at[0, 0]).wait()
    pltpu.make_async_copy(got_b, got_b, sum_sem.at[0, 1]).wait()
    count = n_patch // 2
    while count:
        for ref, sem in ((flux_recv, flux_sem), (back_recv, back_sem)):
            some = ref.at[pl.ds(0, count), :]
            pltpu.make_async_copy(some, some, sem.at[0]).wait()
        count //= 2


def store(a, b, c, a_out, b_out, c_out, sem):
    copies = [pltpu.make_async_copy(x, y, sem.at[i]) for i, (x, y) in enumerate(((a, a_out), (b, b_out), (c, c_out)))]
    for copy in copies:
        copy.start()
    for copy in copies:
        copy.wait()


def solution(mesh):
    dims = tuple(mesh.shape[a] for a in ("sec", "patch", "lev"))
    n_sec, n_patch, n_lev = dims

    def per_device(atm, offs, edge, rates, mixing, owners, weights, mask, ocean, forcing_mix):
        ntr, klev, ncol = atm.shape
        rows, wide = klev + 2 * HALO, ncol + 2 * LANES
        block = ncol // n_lev
        nflux = mixing.shape[0]
        owners, mask = owners.reshape(1, -1), mask.reshape(1, -1)
        dma = pltpu.SemaphoreType.DMA
        vmem = pltpu.VMEM
        any_space = pl.BlockSpec(memory_space=pltpu.HBM)
        in_vmem = pl.BlockSpec(memory_space=pltpu.VMEM)
        operands = [
            pltpu.with_memory_space_constraint(x, pltpu.HBM)
            for x in (atm, offs, edge, rates, mixing, owners, weights, mask, ocean, forcing_mix)
        ]
        out = pl.pallas_call(
            functools.partial(interval, dims),
            out_shape=(
                jax.ShapeDtypeStruct(atm.shape, F32),
                jax.ShapeDtypeStruct(ocean.shape, F32),
                jax.ShapeDtypeStruct((1, block), F32),
            ),
            in_specs=[any_space] * 10,
            out_specs=(in_vmem,) * 3,
            scratch_shapes=[
                vmem((ntr, rows, wide), F32),
                vmem((rows, wide), F32),
                vmem((5, 8, wide), F32),
                vmem(offs.shape, jnp.int32),
                vmem(edge.shape, F32),
                pltpu.SMEM(rates.shape, F32),
                vmem(mixing.shape, F32),
                vmem(owners.shape, jnp.int32),
                vmem(weights.shape, BF16),
                vmem(mask.shape, jnp.int32),
                vmem(ocean.shape, F32),
                vmem(ocean.shape, F32),
                vmem(forcing_mix.shape, F32),
                vmem((2, 3, 8, LANES), F32),
                vmem((2, 5, 8, LANES), F32),
                vmem((2, 4, 8, LANES), F32),
                vmem((2, klev, LANES), F32),
                vmem((n_lev, block // LANES, 8, LANES), F32),
                vmem((n_lev, block // LANES, ntr - 8, LANES), F32),
                vmem((n_lev - 1, block // LANES, 8, LANES), F32),
                vmem((n_lev - 1, block // LANES, ntr - 8, LANES), F32),
                vmem((n_patch, 2 * LANES), F32),
                vmem((n_patch, 2 * LANES), F32),
                vmem((weights.shape[0] // LANES, LANES), F32),
                vmem((n_patch, LANES), F32),
                vmem((n_patch, block), F32),
                vmem((LANES, block), BF16),
                vmem((ntr, nflux, block), F32),
                dma((ntr,)),
                dma((9,)),
                dma((3,)),
                pltpu.SemaphoreType.REGULAR,
                dma((2, ntr)),
                dma((ntr,)),
                dma((ntr,)),
                dma((2, 2)),
                dma((2,)),
                dma((2,)),
            ],
            compiler_params=pltpu.CompilerParams(
                collective_id=0, has_side_effects=True, vmem_limit_bytes=40 * 1024 * 1024
            ),
            name="interval",
        )(*operands)
        out = pl.pallas_call(
            store,
            out_shape=tuple(jax.ShapeDtypeStruct(x.shape, F32) for x in out),
            in_specs=[in_vmem] * 3,
            out_specs=(any_space,) * 3,
            scratch_shapes=[dma((3,))],
            compiler_params=pltpu.CompilerParams(vmem_limit_bytes=8 * 1024 * 1024),
            name="store",
        )(*out)
        return out[0], out[1], out[2].reshape(-1)

    in_specs = (
        P(None, "lev", ("sec", "patch")),
        P(None, ("sec", "patch")),
        P(None, ("sec", "patch")),
        P(),
        P(),
        P(("sec", "patch", "lev"), None),
        P(None, ("sec", "patch", "lev")),
        P(("sec", "patch", "lev")),
        P(None, None, ("sec", "patch", "lev")),
        P(),
    )
    out_specs = (
        P(None, "lev", ("sec", "patch")),
        P(None, None, ("sec", "patch", "lev")),
        P(("sec", "patch", "lev")),
    )
    return jax.shard_map(per_device, mesh=mesh, in_specs=in_specs, out_specs=out_specs, check_vma=False)
```

```python
import functools
import jax
import jax.numpy as jnp
from jax import lax
from jax.experimental import pallas as pl
from jax.experimental.pallas import tpu as pltpu
from jax.sharding import PartitionSpec as P

F32 = jnp.float32
BF16 = jnp.bfloat16
MESH = pl.DeviceIdType.MESH
DELTAS = (-2, -1, 1, 2)
LANES = 128
HALO = 4
GROUP = 3 * HALO


def split_2(x):
    high = x.astype(BF16)
    return high, (x - high.astype(F32)).astype(BF16)


def interval(
    dims,
    atm, offs, edge, rates, mixing, owners, weights, mask, ocean, forcing_mix,
    result, ocean_new, surface_new,
    ring, step1, coef, offs_v, edge_v, rates_s, mix_v, owners_v, weights_v, mask_v, ocean_v, base_v, fmix_v,
    edge_send, edge_recv, own_edge, outer_v, sums_a, sums_b, got_a, got_b, flux_send, flux_recv, back_send, back_recv,
    cols_hot, slot_hot, mix_cols,
    atm_sem, border_sem, in_sem, edge_sem, answer_sem, lev_send_sem, lev_up_sem, lev_down_sem, sum_sem, flux_sem, back_sem,
):
    n_sec, n_patch, n_lev = dims
    ntr, klev, ncol = atm.shape
    alev = klev * n_lev
    block = ncol // n_lev
    slots = weights.shape[0] // n_patch
    copies = LANES // slots
    wide = ncol + 2 * LANES
    rows = klev + 2 * HALO

    sec, patch, lev = lax.axis_index("sec"), lax.axis_index("patch"), lax.axis_index("lev")
    place = sec * n_patch + patch
    n_place = n_sec * n_patch

    def column_neighbour(step):
        other = lax.rem(place + step + n_place, n_place)
        return lax.div(other, n_patch), lax.rem(other, n_patch)

    def beside(side):
        s, p = column_neighbour(2 * side - 1)
        return s, p, s < sec, s > sec

    def level_of(step):
        return lax.rem(lev + step + n_lev, n_lev)

    small = [
        (offs, offs_v), (edge, edge_v), (rates, rates_s), (owners, owners_v),
        (mixing, mix_v), (forcing_mix, fmix_v), (mask, mask_v), (ocean, ocean_v), (weights, weights_v),
    ]
    loads = [pltpu.make_async_copy(a, b, in_sem.at[i]) for i, (a, b) in enumerate(small)]
    for i in (0, 1):
        loads[i].start()
    border_loads = [
        pltpu.make_async_copy(
            atm.at[:, :, at : at + LANES], ring.at[:, 0:klev, LANES + at : 2 * LANES + at], border_sem.at[i]
        )
        for i, at in enumerate((0, ncol - LANES))
    ]
    atm_loads = [
        pltpu.make_async_copy(
            atm.at[t, :, LANES : ncol - LANES], ring.at[t, 0:klev, 2 * LANES : ncol], atm_sem.at[t]
        )
        for t in range(ntr)
    ]
    for load in border_loads + atm_loads:
        load.start()

    barrier = pltpu.get_barrier_semaphore()

    def greet(where):
        pl.semaphore_signal(barrier, inc=1, device_id=where, device_id_type=MESH)

    first_opens = (sec > 0).astype(jnp.int32)
    last_opens = (sec == n_sec - 1).astype(jnp.int32) if n_sec > 1 else jnp.int32(0)

    def opens(p):
        return ((p == 0) & (first_opens == 1)) | ((p == n_patch - 1) & (last_opens == 1))

    opener = opens(patch)
    openers_beside = first_opens * last_opens
    expected = (n_lev - 1) + jnp.where(opener, openers_beside, n_patch - 1)
    for side in range(2):
        s, p, lower, higher = beside(side)
        same = jnp.logical_not(lower | higher)

        @pl.when(higher | (same & (opener | jnp.logical_not(opens(p)))))
        def _(s=s, p=p):
            for step in (-1, 0, 1):
                greet((s, p, level_of(step)))

        expected = expected + jnp.where(lower | (same & jnp.logical_not(opener)), 3, 0)
    for i in range(1, n_lev):
        greet((sec, patch, level_of(i)))

    def greet_patch(i, carry):
        other = lax.rem(patch + i, n_patch)

        @pl.when(jnp.logical_not(opens(other)))
        def _():
            greet((sec, other, lev))

        return carry

    for p in (0, n_patch - 1):
        @pl.when(opener & opens(jnp.int32(p)) & (patch != p))
        def _(p=p):
            greet((sec, p, lev))

    @pl.when(jnp.logical_not(opener))
    def _():
        lax.fori_loop(1, n_patch, greet_patch, 0)

    for load in loads[2:]:
        load.start()

    loads[0].wait()
    loads[1].wait()
    offsets, exchange = offs_v[...], edge_v[...]
    total = jnp.zeros((1, ncol), F32)
    for i, delta in enumerate(DELTAS):
        part = jnp.sum(jnp.where(offsets == delta, exchange, 0.0), axis=0, keepdims=True)
        total = total + part
        coef[i, :, LANES : LANES + ncol] = jnp.broadcast_to(part, (8, ncol))
    coef[4, :, LANES : LANES + ncol] = jnp.broadcast_to(1.0 - total, (8, ncol))

    lane = lax.broadcasted_iota(jnp.int32, (8, LANES), 1)
    row = lax.broadcasted_iota(jnp.int32, (8, LANES), 0)
    for load in border_loads:
        load.wait()

    def packed(of_tracer, source, width, target):
        out = jnp.zeros((8, LANES), F32)
        for t in range(ntr):
            at = GROUP * t + target
            shift = (at - source) % LANES
            x = of_tracer(t)
            out = jnp.where((lane >= at) & (lane < at + width), pltpu.roll(x, shift, 1) if shift else x, out)
        return out

    starts = (LANES, ncol)
    coef_rows = []
    for start in starts:
        out = jnp.zeros((8, LANES), F32)
        for i in range(4):
            out = jnp.where(row == i, coef[i, :, start : start + LANES], out)
        coef_rows.append(out)

    def at_border(side, k, source, width, target):
        if k == 3:
            return packed(lambda t: coef_rows[side], source, width, target)
        start = starts[side]
        return packed(lambda t: ring[t, 8 * k : 8 * k + 8, start : start + LANES], source, width, target)

    for i, k in enumerate((0, 1, 3)):
        edge_send[0, i] = at_border(0, k, 0, HALO, 2 * HALO)
        edge_send[1, i] = at_border(1, k, LANES - HALO, HALO, 0)
    own_edge[0, 3] = at_border(0, 3, 0, 2 * HALO, HALO)
    own_edge[1, 3] = at_border(1, 3, LANES - 2 * HALO, 2 * HALO, 0)

    pl.semaphore_wait(barrier, expected)

    def send_edge(side):
        s, p, _, _ = beside(side)
        away, there = edge_send.at[side], edge_recv.at[1 - side]
        for step, src, dst in (
            (0, away, there.at[0:3]),
            (1, away.at[1], there.at[3]),
            (-1, away.at[0], there.at[4]),
        ):
            pltpu.make_async_remote_copy(
                src_ref=src,
                dst_ref=dst,
                send_sem=edge_sem.at[0],
                recv_sem=edge_sem.at[2 - side],
                device_id=(s, p, level_of(step)),
                device_id_type=MESH,
            ).start()

    def answer(where):
        pl.semaphore_signal(answer_sem, inc=1, device_id=where, device_id_type=MESH)

    for side in range(2):
        s, p, lower, higher = beside(side)
        same = jnp.logical_not(lower | higher)

        @pl.when(lower | (same & jnp.logical_not(opener)))
        def _(side=side):
            send_edge(side)

        @pl.when(same & jnp.logical_not(opener) & opens(p))
        def _(s=s, p=p):
            for step in (-1, 0, 1):
                answer((s, p, level_of(step)))

    @pl.when(opener)
    def _():
        lax.fori_loop(1, n_patch, greet_patch, 0)

    for p in (0, n_patch - 1):
        @pl.when(jnp.logical_not(opener) & opens(jnp.int32(p)))
        def _(p=p):
            answer((sec, p, lev))

    def to_lower(t):
        return pltpu.make_async_remote_copy(
            src_ref=atm.at[t, 0:HALO, :],
            dst_ref=ring.at[t, klev : klev + HALO, LANES : LANES + ncol],
            send_sem=lev_send_sem.at[0, t],
            recv_sem=lev_up_sem.at[t],
            device_id=(sec, patch, level_of(-1)),
            device_id_type=MESH,
        )

    def to_upper(t):
        return pltpu.make_async_remote_copy(
            src_ref=atm.at[t, klev - HALO : klev, :],
            dst_ref=ring.at[t, klev + HALO : rows, LANES : LANES + ncol],
            send_sem=lev_send_sem.at[1, t],
            recv_sem=lev_down_sem.at[t],
            device_id=(sec, patch, level_of(1)),
            device_id_type=MESH,
        )

    @pl.when(lev > 0)
    def _():
        for t in range(ntr):
            to_lower(t).start()

    @pl.when(lev < n_lev - 1)
    def _():
        for t in range(ntr):
            to_upper(t).start()

    @pl.when(lev == 0)
    def _():
        ring[:, klev + HALO : rows, LANES : LANES + ncol] = jnp.zeros((ntr, HALO, ncol), F32)

    @pl.when(lev == n_lev - 1)
    def _():
        ring[:, klev : klev + HALO, LANES : LANES + ncol] = jnp.zeros((ntr, HALO, ncol), F32)

    for load in loads[2:] + atm_loads:
        load.wait()
    owned = owners_v[...]
    hot = (lax.broadcasted_iota(jnp.int32, (n_patch, block), 0) == owned).astype(F32)
    cols_hot[...] = hot
    earlier = (
        lax.broadcasted_iota(jnp.int32, (block, block), 0) < lax.broadcasted_iota(jnp.int32, (block, block), 1)
    ).astype(F32).astype(BF16)
    rank = jnp.dot(hot.astype(BF16), earlier, preferred_element_type=F32)
    slot = jnp.sum(rank * hot, axis=0, keepdims=True).astype(jnp.int32)
    lane_slot = lax.rem(lax.broadcasted_iota(jnp.int32, (LANES, block), 0), slots)
    slot_hot[...] = (lane_slot == slot).astype(F32).astype(BF16)
    for t in range(ntr):
        mix_cols[t] = jnp.broadcast_to(mix_v[:, t : t + 1], (mixing.shape[0], block))

    state = ocean_v[...]
    nol = state.shape[1]
    level = lax.broadcasted_iota(jnp.int32, state.shape, 1)
    above = jnp.where(level < nol - 1, pltpu.roll(state, nol - 1, 1) - state, 0.0)
    below = jnp.where(level > 0, pltpu.roll(state, 1, 1) - state, 0.0)
    base_v[...] = state + 0.2 * above + 0.2 * below

    @pl.when(opener)
    def _():
        pl.semaphore_wait(answer_sem, n_patch - 1 - openers_beside + 3)
        for side in range(2):
            _, _, lower, higher = beside(side)

            @pl.when(jnp.logical_not(lower | higher))
            def _(side=side):
                send_edge(side)

    ring_row = lax.broadcasted_iota(jnp.int32, (rows, LANES), 0)
    k = lev * klev + jnp.where(ring_row < klev + HALO, ring_row, ring_row - rows)
    inside = (k >= 0) & (k < alev)
    vertical = (
        3.0
        - (k < 1).astype(F32) - 0.5 * (k < 2).astype(F32)
        - (k > alev - 2).astype(F32) - 0.5 * (k > alev - 3).astype(F32)
    )
    inside_halo = inside[klev:, :]

    def across(x, times):
        return jnp.concatenate([x] * times, axis=1) if times > 1 else x

    def down(x):
        return jnp.concatenate([x] * (rows // 8), axis=0)

    def stencil(x, part, centre, sides, rate):
        middle = x[:, part]
        out = middle * centre
        for side, delta in zip(sides, DELTAS):
            out = out + side * pltpu.roll(x, (-delta) % x.shape[1], 1)[:, part]
        one = pltpu.roll(middle, 1, 0) + pltpu.roll(middle, rows - 1, 0)
        two = pltpu.roll(middle, 2, 0) + pltpu.roll(middle, rows - 2, 0)
        return out + rate * (one + 0.5 * two)

    def masked(x, tiles):
        return jnp.concatenate(
            [x[:klev], jnp.where(across(inside_halo, tiles), x[klev:], 0.0)], axis=0
        )

    per_block = block // LANES
    n_a = sums_a.shape[2]
    tiles = 8
    chunk = tiles * LANES

    def step(x, at, rate, rate_vertical):
        columns = slice(at, at + chunk)
        return stencil(
            x,
            slice(LANES, LANES + chunk),
            down(coef[4, :, columns]) - across(rate_vertical, tiles),
            [down(coef[i, :, columns]) for i in range(4)],
            rate,
        )

    def inner(t, sums, at_row):
        @pl.when(lev < n_lev - 1)
        def _():
            to_lower(t).wait_recv()

        @pl.when(lev > 0)
        def _():
            to_upper(t).wait_recv()

        rate = rates_s[t]
        rate_vertical = rate * vertical
        for at in range(LANES, LANES + ncol, chunk):
            x = ring[t, :, at - LANES : at + chunk + LANES]
            step1[:, at : at + chunk] = masked(step(x, at, rate, rate_vertical), tiles)
        for at in range(LANES, LANES + ncol, chunk):
            x = step1[:, at - LANES : at + chunk + LANES]
            out = step(x, at, rate, rate_vertical)[:klev]
            result[t, :, at - LANES : at - LANES + chunk] = out
            column_sums = jnp.sum(out, axis=0, keepdims=True)
            for i in range(tiles):
                d, half = divmod(at // LANES - 1 + i, per_block)
                sums[d, half, pl.ds(at_row, 1), :] = column_sums[:, i * LANES : (i + 1) * LANES]

    def send_sums(d):
        @pl.when(lev != d)
        def _():
            for which, (sums, got) in enumerate(((sums_a, got_a), (sums_b, got_b))):
                pltpu.make_async_remote_copy(
                    src_ref=sums.at[d],
                    dst_ref=got.at[lax.rem(lev - d + n_lev, n_lev) - 1],
                    send_sem=sum_sem.at[0, which],
                    recv_sem=sum_sem.at[1, which],
                    device_id=(sec, patch, d),
                    device_id_type=MESH,
                ).start()

    def all_tracers(step):
        def with_a(t, carry):
            step(t, sums_a, t)
            return carry

        def with_b(t, carry):
            step(t, sums_b, t - n_a)
            return carry

        lax.fori_loop(0, n_a, with_a, 0)
        lax.fori_loop(n_a, ntr, with_b, 0)

    all_tracers(inner)
    for d in range(1, n_lev - 1):
        send_sums(d)

    for k in range(3):
        own_edge[0, k] = at_border(0, k, 0, 2 * HALO, HALO)
        own_edge[1, k] = at_border(1, k, LANES - 2 * HALO, 2 * HALO, 0)
    in_group = lane
    lane_rate = jnp.zeros((8, LANES), F32)
    for t in range(ntr):
        here = lane >= GROUP * t
        in_group = jnp.where(here, lane - GROUP * t, in_group)
        lane_rate = jnp.where(here, rates_s[t], lane_rate)
    lane_rate = down(lane_rate)
    lane_vertical = lane_rate * vertical

    def one_side(i, carry):
        side = lax.rem(i + (patch == 0).astype(jnp.int32), 2)
        here = edge_recv.at[side]
        pltpu.make_async_copy(here, here, edge_sem.at[1 + side]).wait()

        theirs = (in_group < HALO * (1 - side)) | (in_group >= GROUP - HALO * side)
        corner = jnp.where(row < HALO, edge_recv[side, 4], edge_recv[side, 3])
        x = jnp.concatenate(
            [
                jnp.where(theirs, edge_recv[side, 0], own_edge[side, 0]),
                jnp.where(theirs, edge_recv[side, 1], own_edge[side, 1]),
                jnp.where(inside_halo, jnp.where(theirs, corner, own_edge[side, 2]), 0.0),
            ],
            axis=0,
        )
        factors = jnp.where(theirs, edge_recv[side, 2], own_edge[side, 3])
        sides = [factors[k : k + 1, :] for k in range(4)]
        centre = 1.0 - (sides[0] + sides[1] + sides[2] + sides[3]) - lane_vertical
        for last in (False, True):
            x = stencil(x, slice(0, LANES), centre, sides, lane_rate)
            if not last:
                x = masked(x, 1)
        out = x[:klev]
        outer_v[side] = out
        column_sums = jnp.broadcast_to(jnp.sum(out, axis=0, keepdims=True), (8, LANES))
        first_lane = side * (LANES - HALO)
        changed = (lane >= first_lane) & (lane < first_lane + HALO)
        d, half = side * (n_lev - 1), side * (per_block - 1)
        for sums, t0, t1 in ((sums_a, 0, n_a), (sums_b, n_a, ntr)):
            values = jnp.zeros((8, LANES), F32)
            for t in range(t0, t1):
                values = jnp.where(row == t - t0, pltpu.roll(column_sums, (-GROUP * t - HALO) % LANES, 1), values)
            values = jnp.where(changed, pltpu.roll(values, first_lane, 1), 0.0)
            sums[d, half] = jnp.where(changed[: t1 - t0], values[: t1 - t0], sums[d, half])
        send_sums(d)

        @pl.when(beside(side)[3])
        def _():
            send_edge(side)

        return carry

    lax.fori_loop(0, 2, one_side, 0)
    lane_of_two = lax.broadcasted_iota(jnp.int32, (klev, LANES), 1)
    for side in range(2):
        out = outer_v[side]
        first_lane = side * (LANES - HALO)
        changed = (lane_of_two >= first_lane) & (lane_of_two < first_lane + HALO)
        columns = slice(side * (ncol - LANES), side * (ncol - LANES) + LANES)
        for t in range(ntr):
            shift = (first_lane - GROUP * t - HALO) % LANES
            result[t, :, columns] = jnp.where(changed, pltpu.roll(out, shift, 1), result[t, :, columns])

    pick = (
        lax.broadcasted_iota(jnp.int32, (ntr, ntr), 0) == lax.broadcasted_iota(jnp.int32, (ntr, ntr), 1)
    )
    fmix = fmix_v[...]
    fmix_cols = [
        jnp.sum(jnp.where(pick, jnp.broadcast_to(fmix[v : v + 1, :], (ntr, ntr)), 0.0), axis=1, keepdims=True)
        for v in range(2)
    ]

    def level_sums(sums, got, which):
        pltpu.make_async_copy(got, got, sum_sem.at[1, which]).wait()
        out = sums[lev]
        for i in range(n_lev - 1):
            out = out + got[i]
        return jnp.concatenate([out[i] for i in range(per_block)], axis=1)

    mean_a = level_sums(sums_a, got_a, 0) * (1.0 / alev)
    mixed = jnp.zeros((mixing.shape[0], block), F32)
    for t in range(n_a):
        mixed = mixed + mix_cols[t] * mean_a[t : t + 1, :]
    mean_b = level_sums(sums_b, got_b, 1) * (1.0 / alev)
    for t in range(n_a, ntr):
        mixed = mixed + mix_cols[t] * mean_b[t - n_a : t - n_a + 1, :]
    flux = jnp.tanh(mixed)
    hot = cols_hot[...]
    parts = []
    for v in range(2):
        forced = jnp.sum(fmix_cols[v] * flux, axis=0, keepdims=True)
        parts += [(hot * piece.astype(F32)).astype(BF16) for piece in split_2(forced)]
    slot_map = slot_hot[...]
    out = lax.dot_general(
        jnp.concatenate(parts, axis=0), slot_map, (((1,), (1,)), ((), ())), preferred_element_type=F32
    )
    outgoing = [out[2 * v * n_patch : (2 * v + 1) * n_patch] + out[(2 * v + 1) * n_patch : (2 * v + 2) * n_patch] for v in range(2)]
    for v in range(2):
        flux_send[:, v * LANES : (v + 1) * LANES] = outgoing[v]

    across_patch = 4
    down_patch = n_patch // across_patch

    def far_first(i):
        def moved(i, n):
            half = lax.div(i + 1, 2)
            return n // 2 + jnp.where(lax.rem(i, 2) == 1, -half, half)

        y = lax.div(patch, across_patch) + moved(lax.div(i, across_patch), down_patch)
        x = lax.rem(patch, across_patch) + moved(lax.rem(i, across_patch), across_patch)
        return lax.rem(y, down_patch) * across_patch + lax.rem(x, across_patch)

    def send_flux(i, carry):
        other = far_first(i)
        pltpu.make_async_remote_copy(
            src_ref=flux_send.at[pl.ds(other, 1), :],
            dst_ref=flux_recv.at[pl.ds(patch, 1), :],
            send_sem=flux_sem.at[0],
            recv_sem=flux_sem.at[1],
            device_id=(sec, other, lev),
            device_id_type=MESH,
        ).start()
        return carry

    lax.fori_loop(0, n_patch - 1, send_flux, 0)
    own_row = pl.ds(patch, 1)
    pltpu.make_async_copy(flux_send.at[own_row, :], flux_recv.at[own_row, :], flux_sem.at[1]).start()
    ocean_cells = mask_v[...].astype(F32)
    pltpu.make_async_copy(flux_recv, flux_recv, flux_sem.at[1]).wait()

    groups = n_patch * slots // LANES
    received = []
    for v in range(2):
        pieces = []
        for g in range(groups):
            tile = flux_recv[g * copies : (g + 1) * copies, v * LANES : (v + 1) * LANES]
            pieces.append(jnp.sum(jnp.where(lax.div(lane, slots) == row, tile, 0.0), axis=0, keepdims=True))
        received.append(jnp.concatenate(pieces, axis=1))
    w = weights_v[...]

    def stacked(values):
        at = lax.broadcasted_iota(jnp.int32, (16, values[0].shape[1]), 0)
        out = jnp.zeros((16, values[0].shape[1]), F32)
        for i, value in enumerate(values):
            out = jnp.where(at == i, value.astype(F32), out)
        return out.astype(BF16)

    sums = jnp.dot(stacked([*split_2(received[0]), *split_2(received[1])]), w, preferred_element_type=F32)
    forcing = [(sums[2 * v : 2 * v + 1] + sums[2 * v + 1 : 2 * v + 2]) * ocean_cells for v in range(2)]
    warmth = (base_v[0, 0:1, :] + forcing[0]) * ocean_cells
    back = lax.dot_general(
        stacked([*split_2(warmth)]), w, (((1,), (1,)), ((), ())), preferred_element_type=F32
    )
    back = back[0:1] + back[1:2]
    for g in range(groups):
        back_send[g : g + 1, :] = back[:, g * LANES : (g + 1) * LANES]

    def send_back(i, carry):
        other = far_first(i)
        pltpu.make_async_remote_copy(
            src_ref=back_send.at[pl.ds(lax.div(other, copies), 1), :],
            dst_ref=back_recv.at[pl.ds(patch, 1), :],
            send_sem=back_sem.at[0],
            recv_sem=back_sem.at[1],
            device_id=(sec, other, lev),
            device_id_type=MESH,
        ).start()
        return carry

    lax.fori_loop(0, n_patch - 1, send_back, 0)
    pltpu.make_async_copy(
        back_send.at[pl.ds(lax.div(patch, copies), 1), :], back_recv.at[own_row, :], back_sem.at[1]
    ).start()

    depth = lax.broadcasted_iota(jnp.int32, (nol, block), 0).astype(F32)
    profile = jnp.exp(-depth / 8.0)
    for v in range(2):
        ocean_new[v] = base_v[v] + profile * forcing[v]

    pltpu.make_async_copy(back_recv, back_recv, back_sem.at[1]).wait()
    at_lane = lax.broadcasted_iota(jnp.int32, (n_patch, LANES), 1)
    own = lax.div(at_lane, slots) == lax.rem(patch, copies)
    returned = jnp.where(own, back_recv[...], 0.0)
    values = jnp.dot(jnp.concatenate(split_2(returned), axis=0), slot_map, preferred_element_type=F32)
    surface_new[...] = jnp.sum((values[:n_patch] + values[n_patch:]) * hot, axis=0, keepdims=True)

    pltpu.make_async_copy(edge_recv, edge_recv, edge_sem.at[0]).wait()

    @pl.when(lev > 0)
    def _():
        for t in range(ntr):
            to_lower(t).wait_send()

    @pl.when(lev < n_lev - 1)
    def _():
        for t in range(ntr):
            to_upper(t).wait_send()

    pltpu.make_async_copy(got_a, got_a, sum_sem.at[0, 0]).wait()
    pltpu.make_async_copy(got_b, got_b, sum_sem.at[0, 1]).wait()
    count = n_patch // 2
    while count:
        for ref, sem in ((flux_recv, flux_sem), (back_recv, back_sem)):
            some = ref.at[pl.ds(0, count), :]
            pltpu.make_async_copy(some, some, sem.at[0]).wait()
        count //= 2


def store(a, b, c, a_out, b_out, c_out, sem):
    pairs = [(a.at[t], a_out.at[t]) for t in range(a.shape[0])] + [(b, b_out), (c, c_out)]
    copies = [pltpu.make_async_copy(x, y, sem.at[i]) for i, (x, y) in enumerate(pairs)]
    for copy in copies:
        copy.start()
    for copy in copies:
        copy.wait()


def solution(mesh):
    dims = tuple(mesh.shape[a] for a in ("sec", "patch", "lev"))
    n_sec, n_patch, n_lev = dims

    def per_device(atm, offs, edge, rates, mixing, owners, weights, mask, ocean, forcing_mix):
        ntr, klev, ncol = atm.shape
        rows, wide = klev + 2 * HALO, ncol + 2 * LANES
        block = ncol // n_lev
        nflux = mixing.shape[0]
        owners, mask = owners.reshape(1, -1), mask.reshape(1, -1)
        dma = pltpu.SemaphoreType.DMA
        vmem = pltpu.VMEM
        any_space = pl.BlockSpec(memory_space=pltpu.HBM)
        in_vmem = pl.BlockSpec(memory_space=pltpu.VMEM)
        operands = [
            pltpu.with_memory_space_constraint(x, pltpu.HBM)
            for x in (atm, offs, edge, rates, mixing, owners, weights, mask, ocean, forcing_mix)
        ]
        out = pl.pallas_call(
            functools.partial(interval, dims),
            out_shape=(
                jax.ShapeDtypeStruct(atm.shape, F32),
                jax.ShapeDtypeStruct(ocean.shape, F32),
                jax.ShapeDtypeStruct((1, block), F32),
            ),
            in_specs=[any_space] * 10,
            out_specs=(in_vmem,) * 3,
            scratch_shapes=[
                vmem((ntr, rows, wide), F32),
                vmem((rows, wide), F32),
                vmem((5, 8, wide), F32),
                vmem(offs.shape, jnp.int32),
                vmem(edge.shape, F32),
                pltpu.SMEM(rates.shape, F32),
                vmem(mixing.shape, F32),
                vmem(owners.shape, jnp.int32),
                vmem(weights.shape, BF16),
                vmem(mask.shape, jnp.int32),
                vmem(ocean.shape, F32),
                vmem(ocean.shape, F32),
                vmem(forcing_mix.shape, F32),
                vmem((2, 3, 8, LANES), F32),
                vmem((2, 5, 8, LANES), F32),
                vmem((2, 4, 8, LANES), F32),
                vmem((2, klev, LANES), F32),
                vmem((n_lev, block // LANES, 8, LANES), F32),
                vmem((n_lev, block // LANES, ntr - 8, LANES), F32),
                vmem((n_lev - 1, block // LANES, 8, LANES), F32),
                vmem((n_lev - 1, block // LANES, ntr - 8, LANES), F32),
                vmem((n_patch, 2 * LANES), F32),
                vmem((n_patch, 2 * LANES), F32),
                vmem((weights.shape[0] // LANES, LANES), F32),
                vmem((n_patch, LANES), F32),
                vmem((n_patch, block), F32),
                vmem((LANES, block), BF16),
                vmem((ntr, nflux, block), F32),
                dma((ntr,)),
                dma((2,)),
                dma((9,)),
                dma((3,)),
                pltpu.SemaphoreType.REGULAR,
                dma((2, ntr)),
                dma((ntr,)),
                dma((ntr,)),
                dma((2, 2)),
                dma((2,)),
                dma((2,)),
            ],
            compiler_params=pltpu.CompilerParams(
                collective_id=0, has_side_effects=True, vmem_limit_bytes=40 * 1024 * 1024
            ),
            name="interval",
        )(*operands)
        out = pl.pallas_call(
            store,
            out_shape=tuple(jax.ShapeDtypeStruct(x.shape, F32) for x in out),
            in_specs=[in_vmem] * 3,
            out_specs=(any_space,) * 3,
            scratch_shapes=[dma((ntr + 2,))],
            compiler_params=pltpu.CompilerParams(vmem_limit_bytes=8 * 1024 * 1024),
            name="store",
        )(*out)
        return out[0], out[1], out[2].reshape(-1)

    in_specs = (
        P(None, "lev", ("sec", "patch")),
        P(None, ("sec", "patch")),
        P(None, ("sec", "patch")),
        P(),
        P(),
        P(("sec", "patch", "lev"), None),
        P(None, ("sec", "patch", "lev")),
        P(("sec", "patch", "lev")),
        P(None, None, ("sec", "patch", "lev")),
        P(),
    )
    out_specs = (
        P(None, "lev", ("sec", "patch")),
        P(None, None, ("sec", "patch", "lev")),
        P(("sec", "patch", "lev")),
    )
    return jax.shard_map(per_device, mesh=mesh, in_specs=in_specs, out_specs=out_specs, check_vma=False)
```
